512 devices in a mesh: dp: 32 (over x, y), seq: 16 (over z, core).
Axes of the slice: x: 4, y: 8, z: 8, core: 2. Of those that a mesh axis runs over, the one named last changes fastest.
Arguments:
- volume: bfloat16 [32, 3072, 1024], P('dp', 'seq')
- cotangent: bfloat16 [32, 3072, 1024], P('dp', 'seq'), may hold values from -6 to 6
- weights: bfloat16 [1024, 3, 1024], P('dp')
- pairs: int32 [32, 16, 24, 4], P('dp', 'seq'), may hold values from 0 to 23, as said below
- valid: int32 [32, 16, 24, 4], P('dp', 'seq'), may hold values from 0 to 1, as said below
Outputs:
- attended: bfloat16 [32, 3072, 1024], P('dp', 'seq')
- weight_grad: float32 [1024, 3, 1024], P('dp', None, 'seq')
The draws below stay inside these ranges and needn't reach their ends.
Inputs may be any that keep to these rules, and one draw needn't show every extreme that they name: `pairs`: slot 0 of query block b holds b; the key blocks of one query block's slots are distinct. `valid`: slot 0 is always 1.
All inputs are finite; a program needn't handle non-finite values.
Results may differ from the reference program's by a relative error of at most 0.03.
Values may be sent and summed in bfloat16 or wider, within the bound.
No kernel may reach another device: no remote copies, remote signals or barrier semaphores. Data moves between devices by JAX's collectives and lax.ppermute only.
A program may use at most 64 MiB of HBM per device.

```python
import math
import jax
import jax.numpy as jnp
from jax import lax

D = 1024
H = 16
HD = 64
KS = 4
VOLUMES = 32
SEQ = 3072
NB = 24


def draw_volume(key, part):
    noise_key = jax.random.fold_in(key, 1)
    return jax.random.normal(noise_key, (VOLUMES, SEQ, D), jnp.float32).astype(jnp.bfloat16)


def draw_weights(key, part):
    first_key = jax.random.fold_in(key, 3)
    second_key = jax.random.fold_in(key, 4)
    third_key = jax.random.fold_in(key, 5)
    first_part = jax.random.normal(first_key, (D, H * HD), jnp.float32)
    second_part = jax.random.normal(second_key, (D, H * HD), jnp.float32)
    third_part = jax.random.normal(third_key, (D, H * HD), jnp.float32)
    key_part = second_part
    stacked = jnp.stack([first_part, key_part, third_part], axis=1) * D ** (-0.5)
    return stacked.astype(jnp.bfloat16)


def draw_pairs(key, part):
    perm_key = jax.random.fold_in(key, 6)
    count_all = VOLUMES * H * NB
    key_list = jax.random.split(perm_key, count_all)
    shuffled = jax.vmap(lambda single_key: jax.random.permutation(single_key, NB - 1))(key_list)[:, :KS - 1]
    block_of_row = (jnp.arange(count_all, dtype=jnp.int32) % NB)[:, None]
    others = (block_of_row + 1 + shuffled.astype(jnp.int32)) % NB
    joined = jnp.concatenate([block_of_row, others], axis=1)
    return joined.reshape(VOLUMES, H, NB, KS).astype(jnp.int32)


def draw_valid(key, part):
    rate_key = jax.random.fold_in(key, 7)
    coin_key = jax.random.fold_in(key, 8)
    threshold = jax.random.randint(rate_key, (VOLUMES, H, 1, 1), 1, 9)
    coins = jax.random.randint(coin_key, (VOLUMES, H, NB, KS), 0, 8)
    live_slots = (coins < threshold).astype(jnp.int32)
    return live_slots.at[:, :, :, 0].set(1)


def levels(key, shape, cuts, least, top_value):
    loudness = 1.0
    for axis_at, shards_of in cuts:
        steps = jax.random.uniform(jax.random.fold_in(jax.random.fold_in(key, 6), axis_at), (shards_of,), jnp.float32, least / len(cuts), top_value / len(cuts))
        loudness = loudness * jnp.repeat(jnp.exp(steps), shape[axis_at] // shards_of).reshape((-1,) + (1,) * (len(shape) - 1 - axis_at))
    return loudness


def gaussian(stream_key, shape, deviation, limit, cuts=(), held_as=jnp.bfloat16):
    level = levels(stream_key, shape, cuts, -0.22, 0.18) if cuts else 1.0
    drawn = jax.random.normal(stream_key, shape, jnp.float32) * deviation * level
    return jnp.minimum(jnp.maximum(drawn, -limit), limit).astype(held_as)


def setup_inputs(seed: int = 0) -> dict:
    key_of = jax.random.split(jax.random.key(seed), 6)
    return {
        "volume": draw_volume(jax.random.fold_in(key_of[5], 71), 0),
        "cotangent": gaussian(key_of[1], (VOLUMES, SEQ, H * HD), 1.0, 6.0, ((0, 32), (1, 16))),
        "weights": draw_weights(jax.random.fold_in(key_of[5], 71), 0),
        "pairs": draw_pairs(jax.random.fold_in(key_of[5], 71), 0),
        "valid": draw_valid(jax.random.fold_in(key_of[5], 71), 0),
    }


def head_pass(queries, keys_all, values_all, upstream, pair_list, pair_live):
    block_count, slot_count = pair_list.shape
    all_rows, head_size = queries.shape
    block_rows = all_rows // block_count
    per_step = math.gcd(block_count, max(1, 512 // block_rows))
    steps_n = block_count // per_step
    scaling = head_size ** -0.5
    key_blocks = keys_all.reshape(block_count, block_rows, head_size)
    value_blocks = values_all.reshape(block_count, block_rows, head_size)
    block_index = jnp.arange(block_count, dtype=jnp.int32)

    def step(totals, sliced):
        key_total, value_total = totals
        query_rows, grad_rows, slot_blocks, slot_live = sliced
        key_rows = key_blocks[slot_blocks].reshape(per_step, slot_count * block_rows, head_size)
        value_rows = value_blocks[slot_blocks].reshape(per_step, slot_count * block_rows, head_size)
        live_cols = jnp.repeat(slot_live > 0, block_rows, axis=1)[:, None, :]
        scores = jnp.einsum('nqd,nkd->nqk', query_rows, key_rows, preferred_element_type=jnp.float32) * scaling
        row_max = jnp.max(jnp.where(live_cols, scores, -1e30), axis=-1, keepdims=True)
        exponent = jnp.where(live_cols, jnp.exp(scores - row_max), 0.0)
        prob_full = exponent / jnp.sum(exponent, axis=-1, keepdims=True)
        rounded = prob_full.astype(jnp.bfloat16)
        result = jnp.einsum('nqk,nkd->nqd', rounded, value_rows, preferred_element_type=jnp.float32).astype(jnp.bfloat16)
        value_grad = jnp.einsum('nqk,nqd->nkd', rounded, grad_rows, preferred_element_type=jnp.float32)
        prob_grad = jnp.einsum('nqd,nkd->nqk', grad_rows, value_rows, preferred_element_type=jnp.float32)
        row_dot = jnp.sum(grad_rows.astype(jnp.float32) * result.astype(jnp.float32), axis=-1, keepdims=True)
        score_grad = (prob_full * (prob_grad - row_dot) * scaling).astype(jnp.bfloat16)
        query_grad = jnp.einsum('nqk,nkd->nqd', score_grad, key_rows, preferred_element_type=jnp.float32).astype(jnp.bfloat16)
        key_grad = jnp.einsum('nqk,nqd->nkd', score_grad, query_rows, preferred_element_type=jnp.float32)
        one_hot = ((slot_blocks.reshape(-1)[:, None] == block_index[None, :]) & (slot_live.reshape(-1)[:, None] > 0)).astype(jnp.float32)
        key_total = key_total + jnp.einsum('jb,jrd->brd', one_hot, key_grad.reshape(per_step * slot_count, block_rows, head_size), precision=lax.Precision.HIGHEST)
        value_total = value_total + jnp.einsum('jb,jrd->brd', one_hot, value_grad.reshape(per_step * slot_count, block_rows, head_size), precision=lax.Precision.HIGHEST)
        return (key_total, value_total), (result, query_grad)

    empty_acc = jnp.zeros((block_count, block_rows, head_size), jnp.float32)
    sliced_all = (queries.reshape(steps_n, per_step, block_rows, head_size),
                  upstream.reshape(steps_n, per_step, block_rows, head_size),
                  pair_list.reshape(steps_n, per_step, slot_count),
                  pair_live.reshape(steps_n, per_step, slot_count))
    (key_total, value_total), (results, query_grads) = lax.scan(step, (empty_acc, empty_acc), sliced_all)
    return (results.reshape(all_rows, head_size), query_grads.reshape(all_rows, head_size),
            key_total.astype(jnp.bfloat16).reshape(all_rows, head_size),
            value_total.astype(jnp.bfloat16).reshape(all_rows, head_size))


def one_volume(tokens_in, upstream, weight_matrix, pair_list, pair_live):
    seq_len = tokens_in.shape[0]
    projected = jnp.dot(tokens_in, weight_matrix, preferred_element_type=jnp.float32).astype(jnp.bfloat16)
    by_head = jnp.transpose(projected.reshape(seq_len, 3, H, HD), (1, 2, 0, 3))
    grad_by_head = jnp.transpose(upstream.reshape(seq_len, H, HD), (1, 0, 2))

    def per_head(packed):
        return head_pass(packed[0], packed[1], packed[2], packed[3], packed[4], packed[5])

    outputs = lax.map(per_head, (by_head[0], by_head[1], by_head[2], grad_by_head, pair_list, pair_live))
    attended = jnp.transpose(outputs[0], (1, 0, 2)).reshape(seq_len, H * HD)
    grad_flat = jnp.transpose(jnp.stack([outputs[1], outputs[2], outputs[3]], 0), (2, 0, 1, 3)).reshape(seq_len, 3 * H * HD)
    weight_part = lax.dot_general(tokens_in, grad_flat, (((0,), (0,)), ((), ())), preferred_element_type=jnp.float32)
    return attended, weight_part


def reference(volume, cotangent, weights, pairs, valid):
    weight_matrix = weights.reshape(D, 3 * H * HD)

    def scan_step(running, sliced):
        attended, weight_part = one_volume(sliced[0], sliced[1], weight_matrix, sliced[2], sliced[3])
        return running + weight_part, attended

    grad_total, attended = lax.scan(scan_step, jnp.zeros((D, 3 * H * HD), jnp.float32), (volume, cotangent, pairs, valid))
    return attended, grad_total.reshape(D, 3, H * HD)
```

```python
import functools

import jax
import jax.numpy as jnp
from jax import lax
from jax.experimental import pallas as pl
from jax.experimental.pallas import tpu as pltpu
from jax.sharding import PartitionSpec as P

HD = 64
BLOCK = 128
LOG2E = 1.4426950408889634
CHUNKS = 8
UNROLL = 2

NN = (((1,), (0,)), ((), ()))
NT = (((1,), (1,)), ((), ()))


def mm(a, b, dims=NN):
    return lax.dot_general(a, b, dims, preferred_element_type=jnp.float32)


def head_kernel(
    pairs_ref, valid_ref, vol_hbm, w_ref, cot_ref, att_ref, wg_ref,
    vol_ref, kv_ref, kvt_ref, q_ref, do_ref, acc_ref, dt_ref, o_ref, sems,
):
    rows, width = vol_ref.shape
    n_blocks, slots = pairs_ref.shape
    peers, half, _ = cot_ref.shape
    chunk = rows // CHUNKS
    blocks_per = chunk // BLOCK
    scale = HD ** -0.5

    copies = [
        pltpu.make_async_copy(
            vol_hbm.at[pl.ds(c * chunk, chunk)], vol_ref.at[pl.ds(c * chunk, chunk)], sems.at[c]
        )
        for c in range(CHUNKS)
    ]
    for copy in copies:
        copy.start()

    acc_ref[...] = jnp.zeros_like(acc_ref)
    blank = jnp.zeros((half, HD), jnp.bfloat16)
    for s in range(peers):
        both = cot_ref[s]
        do_ref[pl.ds(2 * half * s, half), :] = jnp.concatenate([blank, both[:, :HD]], axis=1)
        do_ref[pl.ds(2 * half * s + half, half), :] = jnp.concatenate([blank, both[:, HD:]], axis=1)

    for c in range(CHUNKS):
        copies[c].wait()
        got = mm(vol_ref[pl.ds(c * chunk, chunk), :], w_ref[...])
        q_ref[pl.ds(c * chunk, chunk), :] = got[:, BLOCK:].astype(jnp.bfloat16)
        keys = got[:, :BLOCK].astype(jnp.bfloat16)
        for b in range(blocks_per):
            one = keys[b * BLOCK:(b + 1) * BLOCK]
            kv_ref[c * blocks_per + b] = one
            kvt_ref[c * blocks_per + b] = one.T

    def block(b):
        at = pl.ds(pl.multiple_of(b * BLOCK, BLOCK), BLOCK)
        names = [pairs_ref[b, j] for j in range(slots)]
        kv = jnp.concatenate([kv_ref[n] for n in names], axis=0)
        kvt = jnp.concatenate([kvt_ref[n] for n in names], axis=1)
        d_out = do_ref[at, :]
        rhs = jnp.concatenate([q_ref[at, :], d_out], axis=0)
        both = mm(kv, rhs, NT)
        scores = both[:, :BLOCK] * (scale * LOG2E)
        prob_grad = both[:, BLOCK:]
        masked = jnp.concatenate(
            [
                jnp.where(valid_ref[b, j] > 0, scores[j * BLOCK:(j + 1) * BLOCK], -jnp.inf)
                for j in range(slots)
            ],
            axis=0,
        )
        top = jnp.max(masked, axis=0, keepdims=True)
        exponent = jnp.exp2(masked - top)
        probs = exponent * (1.0 / jnp.sum(exponent, axis=0, keepdims=True))
        rounded = probs.astype(jnp.bfloat16)
        out_t = mm(kvt[HD:], rounded).astype(jnp.bfloat16)
        out = out_t.astype(jnp.float32).T
        o_ref[at, :] = out.astype(jnp.bfloat16)
        grad_t = d_out.astype(jnp.float32).T[HD:]
        row_dot = jnp.sum(grad_t * out_t.astype(jnp.float32), axis=0, keepdims=True)
        score_grad = (probs * (prob_grad - row_dot)).astype(jnp.bfloat16)
        query_grad = mm(kvt[:HD], score_grad) * scale
        dt_ref[BLOCK:, at] = query_grad.astype(jnp.bfloat16)
        back = mm(jnp.concatenate([score_grad, rounded], axis=1), rhs)
        for j in range(slots):
            acc_ref[names[j]] += back[j * BLOCK:(j + 1) * BLOCK]

    def body(i, carry):
        for u in range(UNROLL):
            block(i * UNROLL + u)
        return carry

    lax.fori_loop(0, n_blocks // UNROLL, body, 0)

    for s in range(peers):
        att_ref[s] = jnp.concatenate(
            [
                o_ref[pl.ds(2 * half * s, half), :],
                o_ref[pl.ds(2 * half * s + half, half), :],
            ],
            axis=1,
        )
    lane = lax.broadcasted_iota(jnp.int32, (BLOCK, BLOCK), 1)
    factor = jnp.where(lane < HD, scale, 1.0)
    for b in range(n_blocks):
        dt_ref[:BLOCK, b * BLOCK:(b + 1) * BLOCK] = (acc_ref[b] * factor).T.astype(jnp.bfloat16)

    owners = wg_ref.shape[0]
    mine = width // owners
    part = 256
    for n in range(width // part):
        got = mm(dt_ref[...], vol_ref[:, n * part:(n + 1) * part])
        kv_part = got[:BLOCK].T.astype(jnp.bfloat16)
        q_part = got[BLOCK:].T.astype(jnp.bfloat16)
        for k in range(part // mine):
            owner = n * (part // mine) + k
            wg_ref[owner, :mine] = kv_part[k * mine:(k + 1) * mine]
            q_rows = q_part[k * mine:(k + 1) * mine]
            wg_ref[owner, mine:] = jnp.concatenate([q_rows[:mine // 2], q_rows[mine // 2:]], axis=1)


def head_call(pairs, valid, vol, w, cot, owners):
    rows, width = vol.shape
    n_blocks = rows // BLOCK
    mine = width // owners
    vmem = functools.partial(pl.BlockSpec, memory_space=pltpu.VMEM)
    smem = functools.partial(pl.BlockSpec, memory_space=pltpu.SMEM)
    return pl.pallas_call(
        head_kernel,
        out_shape=(
            jax.ShapeDtypeStruct(cot.shape, jnp.bfloat16),
            jax.ShapeDtypeStruct((owners, mine + mine // 2, BLOCK), jnp.bfloat16),
        ),
        in_specs=[smem(), smem(), pl.BlockSpec(memory_space=pl.ANY), vmem(), vmem()],
        out_specs=(vmem(), vmem()),
        scratch_shapes=[
            pltpu.VMEM((rows, width), jnp.bfloat16),
            pltpu.VMEM((n_blocks, BLOCK, BLOCK), jnp.bfloat16),
            pltpu.VMEM((n_blocks, BLOCK, BLOCK), jnp.bfloat16),
            pltpu.VMEM((rows, BLOCK), jnp.bfloat16),
            pltpu.VMEM((rows, BLOCK), jnp.bfloat16),
            pltpu.VMEM((n_blocks, BLOCK, BLOCK), jnp.float32),
            pltpu.VMEM((BLOCK + HD, rows), jnp.bfloat16),
            pltpu.VMEM((rows, HD), jnp.bfloat16),
            pltpu.SemaphoreType.DMA((CHUNKS,)),
        ],
        compiler_params=pltpu.CompilerParams(vmem_limit_bytes=40 * 2**20),
        name="head",
    )(pairs, valid, vol, w, cot)


def local(volume, cotangent, weights, pairs, valid):
    peers = lax.axis_size("seq")
    owners = lax.axis_size("dp")
    vol, cot = volume[0], cotangent[0]
    toks, width = vol.shape
    w_rows = weights.shape[0]
    half = toks // 2

    gathered = lax.all_gather(vol, "seq", axis=0, tiled=True)

    column = lax.axis_index("seq") * HD
    mine = lax.dynamic_slice_in_dim(weights, column, HD, axis=2)
    mine = jnp.stack([mine[:, 1], mine[:, 2], mine[:, 0]], axis=1).reshape(-1, BLOCK)
    sent = jnp.broadcast_to(mine[None], (owners, *mine.shape))
    w = lax.all_to_all(sent, "dp", split_axis=0, concat_axis=0, tiled=True)
    w = w.reshape(owners * w_rows, 3 * HD)
    w = jnp.pad(w, ((0, 0), (0, HD)))

    cot = cot.reshape(2, half, peers, HD).transpose(2, 1, 0, 3).reshape(peers, half, 2 * HD)
    cot = lax.all_to_all(cot, "seq", split_axis=0, concat_axis=0, tiled=True)

    att, wg = head_call(pairs[0, 0], valid[0, 0], gathered, w, cot, owners)

    wg = lax.all_to_all(wg, "dp", split_axis=0, concat_axis=0, tiled=True)
    att = lax.all_to_all(att, "seq", split_axis=0, concat_axis=0, tiled=True)
    att = att.reshape(peers, half, 2, HD).transpose(2, 1, 0, 3).reshape(1, toks, peers * HD)
    total = jnp.sum(wg.astype(jnp.float32), axis=0)
    kv = total[:w_rows].reshape(w_rows, 2, HD)
    q = total[w_rows:].reshape(w_rows // 2, 2, HD).transpose(1, 0, 2).reshape(w_rows, 1, HD)
    return att, jnp.concatenate([q, kv], axis=1)


def solution(mesh):
    return jax.shard_map(
        local,
        mesh=mesh,
        in_specs=(
            P("dp", "seq", None),
            P("dp", "seq", None),
            P("dp", None, None),
            P("dp", "seq", None, None),
            P("dp", "seq", None, None),
        ),
        out_specs=(P("dp", "seq", None), P("dp", None, "seq")),
        check_vma=False,
    )
```

```python
import functools

import jax
import jax.numpy as jnp
from jax import lax
from jax.experimental import pallas as pl
from jax.experimental.pallas import tpu as pltpu
from jax.sharding import PartitionSpec as P

HD = 64
BLOCK = 128
LOG2E = 1.4426950408889634
UNROLL = 4

NN = (((1,), (0,)), ((), ()))
NT = (((1,), (1,)), ((), ()))


def mm(a, b, dims=NN):
    return lax.dot_general(a, b, dims, preferred_element_type=jnp.float32)


def attend(n_blocks, slots, pairs_ref, valid_ref, kv_ref, kvt_ref, q_ref, do_ref, acc_ref, dt_ref, o_ref):
    scale = HD ** -0.5

    def row(b):
        return pl.ds(pl.multiple_of(b * BLOCK, BLOCK), BLOCK)

    def group(blocks):
        names = [[pairs_ref[b, j] for j in range(slots)] for b in blocks]
        rhs = [jnp.concatenate([q_ref[row(b), :], do_ref[row(b), :]], axis=0) for b in blocks]
        both = [
            mm(jnp.concatenate([kv_ref[row(n), :] for n in some], axis=0), r, NT)
            for some, r in zip(names, rhs)
        ]
        sent = []
        for b, pair in zip(blocks, both):
            parts = [pair[j * BLOCK:(j + 1) * BLOCK, :BLOCK] * (scale * LOG2E) for j in range(slots)]
            live = [valid_ref[b, j] > 0 for j in range(slots)]
            tops = [
                jnp.where(ok, jnp.max(part, axis=0, keepdims=True), -jnp.inf)
                for ok, part in zip(live, parts)
            ]
            top = functools.reduce(jnp.maximum, tops)
            exponents = [
                jnp.exp2(part - jnp.where(ok, top, jnp.inf)) for ok, part in zip(live, parts)
            ]
            exponent = jnp.concatenate(exponents, axis=0)
            probs = exponent * (1.0 / jnp.sum(exponent, axis=0, keepdims=True))
            weighted = probs * pair[:, BLOCK:]
            row_dot = jnp.sum(weighted, axis=0, keepdims=True)
            score_grad = (weighted - probs * row_dot).astype(jnp.bfloat16)
            sent.append(jnp.concatenate([score_grad, probs.astype(jnp.bfloat16)], axis=1))
        for b, some, pair in zip(blocks, names, sent):
            kvt = jnp.concatenate([kvt_ref[n] for n in some], axis=1)
            mixed = mm(kvt, pair)
            dt_ref[BLOCK:, row(b)] = (mixed[:HD, :BLOCK] * scale).astype(jnp.bfloat16)
            o_ref[row(b), :] = mixed[HD:, BLOCK:].T.astype(jnp.bfloat16)
        for some, pair, r in zip(names, sent, rhs):
            back = mm(pair, r)
            for j in range(slots):
                acc_ref[some[j]] += back[j * BLOCK:(j + 1) * BLOCK]

    def body(i, carry):
        group([i * UNROLL + u for u in range(UNROLL)])
        return carry

    lax.fori_loop(0, n_blocks // UNROLL, body, 0)


def block_places(me, peers):
    core = lax.rem(me, 2)
    chip = lax.div(me, 2)
    chips = peers // 2
    ahead = 1 - 2 * core
    places = [me, me + ahead]
    for k in range(1, chips // 2 + 1):
        back = lax.rem(chip - k * ahead + chips, chips)
        forth = lax.rem(chip + k * ahead + chips, chips)
        places += [2 * back + core, 2 * forth + 1 - core]
        if k < chips // 2:
            places += [2 * back + 1 - core, 2 * forth + core]
    return places


def head_kernel(*refs):
    me_ref, pairs_ref, valid_ref, w_ref, cot_ref = refs[:5]
    (
        att_ref, wg_ref, vol_ref, kv_ref, kvt_ref, q_ref, do_ref, acc_ref, dt_ref, o_ref,
    ) = refs[-10:]
    blocks = refs[5:-10]
    rows, width = vol_ref.shape
    toks = blocks[0].shape[0]
    n_blocks, slots = pairs_ref.shape
    peers, half, _ = cot_ref.shape
    scale = HD ** -0.5

    acc_ref[...] = jnp.zeros_like(acc_ref)
    blank = jnp.zeros((half, HD), jnp.bfloat16)
    for s in range(peers):
        both = cot_ref[s]
        do_ref[pl.ds(2 * half * s, half), :] = jnp.concatenate([blank, both[:, :HD]], axis=1)
        do_ref[pl.ds(2 * half * s + half, half), :] = jnp.concatenate([blank, both[:, HD:]], axis=1)

    for place, block_ref in zip(block_places(me_ref[0], peers), blocks):
        at = pl.ds(pl.multiple_of(place * toks, HD), toks)
        vol_ref[at, :] = block_ref[...]
        got = mm(block_ref[...], w_ref[...])
        q_ref[at, :] = got[:, BLOCK:].astype(jnp.bfloat16)
        kv_ref[at, :] = got[:, :BLOCK].astype(jnp.bfloat16)
    for b in range(n_blocks):
        kvt_ref[b] = kv_ref[b * BLOCK:(b + 1) * BLOCK, :].T

    attend(n_blocks, slots, pairs_ref, valid_ref, kv_ref, kvt_ref, q_ref, do_ref, acc_ref, dt_ref, o_ref)

    for s in range(peers):
        att_ref[s] = jnp.concatenate(
            [
                o_ref[pl.ds(2 * half * s, half), :],
                o_ref[pl.ds(2 * half * s + half, half), :],
            ],
            axis=1,
        )
    lane = lax.broadcasted_iota(jnp.int32, (BLOCK, BLOCK), 1)
    factor = jnp.where(lane < HD, scale, 1.0)
    for b in range(n_blocks):
        dt_ref[:BLOCK, b * BLOCK:(b + 1) * BLOCK] = (acc_ref[b] * factor).T.astype(jnp.bfloat16)

    owners = wg_ref.shape[0]
    mine = width // owners
    part = 256
    for n in range(width // part):
        got = mm(dt_ref[...], vol_ref[:, n * part:(n + 1) * part])
        kv_part = got[:BLOCK].T.astype(jnp.bfloat16)
        q_part = got[BLOCK:].T.astype(jnp.bfloat16)
        for k in range(part // mine):
            owner = n * (part // mine) + k
            wg_ref[owner, :mine] = kv_part[k * mine:(k + 1) * mine]
            q_rows = q_part[k * mine:(k + 1) * mine]
            wg_ref[owner, mine:] = jnp.concatenate([q_rows[:mine // 2], q_rows[mine // 2:]], axis=1)


def head_call(me, pairs, valid, w, cot, blocks, owners):
    toks, width = blocks[0].shape
    rows = toks * len(blocks)
    n_blocks = rows // BLOCK
    mine = width // owners
    vmem = pl.BlockSpec(memory_space=pltpu.VMEM)
    smem = pl.BlockSpec(memory_space=pltpu.SMEM)
    return pl.pallas_call(
        head_kernel,
        out_shape=(
            jax.ShapeDtypeStruct(cot.shape, jnp.bfloat16),
            jax.ShapeDtypeStruct((owners, mine + mine // 2, BLOCK), jnp.bfloat16),
        ),
        in_specs=[smem] * 3 + [vmem] * (2 + len(blocks)),
        out_specs=(vmem, vmem),
        scratch_shapes=[
            pltpu.VMEM((rows, width), jnp.bfloat16),
            pltpu.VMEM((rows, BLOCK), jnp.bfloat16),
            pltpu.VMEM((n_blocks, BLOCK, BLOCK), jnp.bfloat16),
            pltpu.VMEM((rows, BLOCK), jnp.bfloat16),
            pltpu.VMEM((rows, BLOCK), jnp.bfloat16),
            pltpu.VMEM((n_blocks, BLOCK, BLOCK), jnp.float32),
            pltpu.VMEM((BLOCK + HD, rows), jnp.bfloat16),
            pltpu.VMEM((rows, HD), jnp.bfloat16),
        ],
        compiler_params=pltpu.CompilerParams(vmem_limit_bytes=32 * 2**20),
        name="head",
    )(me, pairs, valid, w, cot, *blocks)


def gather(vol):
    peers = lax.axis_size("seq")
    chips = peers // 2
    onward = [
        (2 * z + c, 2 * ((z + 1) % chips) if c == 0 else 2 * ((z - 1) % chips) + 1)
        for z in range(chips)
        for c in range(2)
    ]
    twin = [(i, i ^ 1) for i in range(peers)]

    def swap(x):
        return lax.ppermute(x, "seq", twin)

    own, other = vol, swap(vol)
    blocks = [own, other]
    for k in range(1, chips // 2 + 1):
        own = lax.ppermute(own, "seq", onward)
        blocks += [own, swap(own)]
        if k < chips // 2:
            other = lax.ppermute(other, "seq", onward)
            blocks += [other, swap(other)]
    return blocks


def local(volume, cotangent, weights, pairs, valid):
    peers = lax.axis_size("seq")
    owners = lax.axis_size("dp")
    vol, cot = volume[0], cotangent[0]
    toks, width = vol.shape
    w_rows = weights.shape[0]
    half = toks // 2

    blocks = gather(vol)
    me = lax.axis_index("seq").reshape(1)

    column = lax.axis_index("seq") * HD
    mine = lax.dynamic_slice_in_dim(weights, column, HD, axis=2)
    mine = jnp.stack([mine[:, 1], mine[:, 2], mine[:, 0]], axis=1).reshape(-1, BLOCK)
    sent = jnp.broadcast_to(mine[None], (owners, *mine.shape))
    w = lax.all_to_all(sent, "dp", split_axis=0, concat_axis=0, tiled=True)
    w = w.reshape(owners * w_rows, 3 * HD)
    w = jnp.pad(w, ((0, 0), (0, HD)))

    cot = cot.reshape(2, half, peers, HD).transpose(2, 1, 0, 3).reshape(peers, half, 2 * HD)
    cot = lax.all_to_all(cot, "seq", split_axis=0, concat_axis=0, tiled=True)

    att, wg = head_call(me, pairs[0, 0], valid[0, 0], w, cot, blocks, owners)

    wg = lax.all_to_all(wg, "dp", split_axis=0, concat_axis=0, tiled=True)
    att = lax.all_to_all(att, "seq", split_axis=0, concat_axis=0, tiled=True)
    att = att.reshape(peers, half, 2, HD).transpose(2, 1, 0, 3).reshape(1, toks, peers * HD)
    total = jnp.sum(wg.astype(jnp.float32), axis=0)
    kv = total[:w_rows].reshape(w_rows, 2, HD)
    q = total[w_rows:].reshape(w_rows // 2, 2, HD).transpose(1, 0, 2).reshape(w_rows, 1, HD)
    return att, jnp.concatenate([q, kv], axis=1)


def solution(mesh):
    return jax.shard_map(
        local,
        mesh=mesh,
        in_specs=(
            P("dp", "seq", None),
            P("dp", "seq", None),
            P("dp", None, None),
            P("dp", "seq", None, None),
            P("dp", "seq", None, None),
        ),
        out_specs=(P("dp", "seq", None), P("dp", None, "seq")),
        check_vma=False,
    )
```

```python
import functools

import jax
import jax.numpy as jnp
from jax import lax
from jax.experimental import pallas as pl
from jax.experimental.pallas import tpu as pltpu
from jax.sharding import PartitionSpec as P

HD = 64
BLOCK = 128
LOG2E = 1.4426950408889634
UNROLL = 4
CHUNKS = 8

NN = (((1,), (0,)), ((), ()))
NT = (((1,), (1,)), ((), ()))


def mm(a, b, dims=NN):
    return lax.dot_general(a, b, dims, preferred_element_type=jnp.float32)


def attend(n_blocks, slots, pairs_ref, valid_ref, kv_ref, kvt_ref, q_ref, do_ref, acc_ref, dt_ref, o_ref):
    scale = HD ** -0.5

    def row(b):
        return pl.ds(pl.multiple_of(b * BLOCK, BLOCK), BLOCK)

    def group(blocks):
        names = [[pairs_ref[b, j] for j in range(slots)] for b in blocks]
        rhs = [jnp.concatenate([q_ref[row(b), :], do_ref[row(b), :]], axis=0) for b in blocks]
        both = [
            mm(jnp.concatenate([kv_ref[row(n), :] for n in some], axis=0), r, NT)
            for some, r in zip(names, rhs)
        ]
        sent = []
        for b, pair in zip(blocks, both):
            parts = [pair[j * BLOCK:(j + 1) * BLOCK, :BLOCK] * (scale * LOG2E) for j in range(slots)]
            live = [valid_ref[b, j] > 0 for j in range(slots)]
            tops = [
                jnp.where(ok, jnp.max(part, axis=0, keepdims=True), -jnp.inf)
                for ok, part in zip(live, parts)
            ]
            top = functools.reduce(jnp.maximum, tops)
            exponents = [
                jnp.exp2(part - jnp.where(ok, top, jnp.inf)) for ok, part in zip(live, parts)
            ]
            exponent = jnp.concatenate(exponents, axis=0)
            probs = exponent * (1.0 / jnp.sum(exponent, axis=0, keepdims=True))
            weighted = probs * pair[:, BLOCK:]
            row_dot = jnp.sum(weighted, axis=0, keepdims=True)
            score_grad = (weighted - probs * row_dot).astype(jnp.bfloat16)
            sent.append(jnp.concatenate([score_grad, probs.astype(jnp.bfloat16)], axis=1))
        for b, some, pair in zip(blocks, names, sent):
            kvt = jnp.concatenate([kvt_ref[n] for n in some], axis=1)
            mixed = mm(kvt, pair)
            dt_ref[BLOCK:, row(b)] = (mixed[:HD, :BLOCK] * scale).astype(jnp.bfloat16)
            out = mixed[HD:, BLOCK:]
            o_ref[row(b), :] = jnp.concatenate([out, out], axis=0).T.astype(jnp.bfloat16)
        for some, pair, r in zip(names, sent, rhs):
            back = mm(pair, r)
            for j in range(slots):
                acc_ref[some[j]] += back[j * BLOCK:(j + 1) * BLOCK]

    def body(i, carry):
        group([i * UNROLL + u for u in range(UNROLL)])
        return carry

    lax.fori_loop(0, n_blocks // UNROLL, body, 0)


def head_kernel(
    me_ref, pairs_ref, valid_ref, w_ref, cot_ref, vol_hbm, mine_ref, give_ref, wg_ref,
    vol_ref, kv_ref, kvt_ref, q_ref, do_ref, acc_ref, dt_ref, o_ref, sems,
):
    rows, width = vol_ref.shape
    n_blocks, slots = pairs_ref.shape
    peers, half, _ = cot_ref.shape
    scale = HD ** -0.5
    chunk = rows // CHUNKS
    copies = [
        pltpu.make_async_copy(
            vol_hbm.at[pl.ds(c * chunk, chunk)], vol_ref.at[pl.ds(c * chunk, chunk)], sems.at[c]
        )
        for c in range(CHUNKS)
    ]
    for copy in copies:
        copy.start()

    acc_ref[...] = jnp.zeros_like(acc_ref)
    blank = jnp.zeros((half, HD), jnp.bfloat16)
    for s in range(peers):
        both = cot_ref[s]
        do_ref[pl.ds(2 * half * s, half), :] = jnp.concatenate([blank, both[:, :HD]], axis=1)
        do_ref[pl.ds(2 * half * s + half, half), :] = jnp.concatenate([blank, both[:, HD:]], axis=1)

    for c in range(CHUNKS):
        copies[c].wait()
        at = pl.ds(c * chunk, chunk)
        got = mm(vol_ref[at, :], w_ref[...])
        q_ref[at, :] = got[:, BLOCK:].astype(jnp.bfloat16)
        kv_ref[at, :] = got[:, :BLOCK].astype(jnp.bfloat16)
    for b in range(n_blocks):
        kvt_ref[b] = kv_ref[b * BLOCK:(b + 1) * BLOCK, :].T

    attend(n_blocks, slots, pairs_ref, valid_ref, kv_ref, kvt_ref, q_ref, do_ref, acc_ref, dt_ref, o_ref)

    core = lax.rem(me_ref[0], 2)
    chip = lax.div(me_ref[0], 2)
    chips = peers // 2
    for k in range(chips):
        to = 2 * lax.rem(chip + k, chips)
        for ref, side in ((mine_ref, core), (give_ref, 1 - core)):
            one = o_ref[pl.ds(pl.multiple_of((to + side) * (2 * half), HD), 2 * half), :]
            ref[k] = one
    lane = lax.broadcasted_iota(jnp.int32, (BLOCK, BLOCK), 1)
    factor = jnp.where(lane < HD, scale, 1.0)
    for b in range(n_blocks):
        dt_ref[:BLOCK, b * BLOCK:(b + 1) * BLOCK] = (acc_ref[b] * factor).T.astype(jnp.bfloat16)

    owners = wg_ref.shape[0]
    mine = width // owners
    part = 256
    for n in range(width // part):
        got = mm(dt_ref[...], vol_ref[:, n * part:(n + 1) * part])
        kv_part = got[:BLOCK].T.astype(jnp.bfloat16)
        q_part = got[BLOCK:].T.astype(jnp.bfloat16)
        for k in range(part // mine):
            owner = n * (part // mine) + k
            wg_ref[owner, :mine] = kv_part[k * mine:(k + 1) * mine]
            q_rows = q_part[k * mine:(k + 1) * mine]
            wg_ref[owner, mine:] = jnp.concatenate([q_rows[:mine // 2], q_rows[mine // 2:]], axis=1)


def head_call(me, pairs, valid, w, cot, vol, owners):
    rows, width = vol.shape
    peers, half, _ = cot.shape
    n_blocks = rows // BLOCK
    mine = width // owners
    vmem = pl.BlockSpec(memory_space=pltpu.VMEM)
    smem = pl.BlockSpec(memory_space=pltpu.SMEM)
    piece = jax.ShapeDtypeStruct((peers // 2, 2 * half, BLOCK), jnp.bfloat16)
    return pl.pallas_call(
        head_kernel,
        out_shape=(
            piece,
            piece,
            jax.ShapeDtypeStruct((owners, mine + mine // 2, BLOCK), jnp.bfloat16),
        ),
        in_specs=[smem] * 3 + [vmem] * 2 + [pl.BlockSpec(memory_space=pl.ANY)],
        out_specs=(vmem, vmem, vmem),
        scratch_shapes=[
            pltpu.VMEM((rows, width), jnp.bfloat16),
            pltpu.VMEM((rows, BLOCK), jnp.bfloat16),
            pltpu.VMEM((n_blocks, BLOCK, BLOCK), jnp.bfloat16),
            pltpu.VMEM((rows, BLOCK), jnp.bfloat16),
            pltpu.VMEM((rows, BLOCK), jnp.bfloat16),
            pltpu.VMEM((n_blocks, BLOCK, BLOCK), jnp.float32),
            pltpu.VMEM((BLOCK + HD, rows), jnp.bfloat16),
            pltpu.VMEM((rows, BLOCK), jnp.bfloat16),
            pltpu.SemaphoreType.DMA((CHUNKS,)),
        ],
        compiler_params=pltpu.CompilerParams(vmem_limit_bytes=56 * 2**20),
        name="head",
    )(me, pairs, valid, w, cot, vol)


def merge_kernel(me_ref, mine_ref, got_ref, *out_refs):
    core = lax.rem(me_ref[0], 2)
    toks = mine_ref.shape[1]
    lane = lax.broadcasted_iota(jnp.int32, (toks, BLOCK), 1)
    own = lax.div(lane, HD) == core
    for k, out_ref in enumerate(out_refs):
        out_ref[...] = jnp.where(own, mine_ref[k], got_ref[k])


def merge_call(me, mine, got):
    vmem = pl.BlockSpec(memory_space=pltpu.VMEM)
    return pl.pallas_call(
        merge_kernel,
        out_shape=[jax.ShapeDtypeStruct(mine.shape[1:], mine.dtype)] * mine.shape[0],
        in_specs=[pl.BlockSpec(memory_space=pltpu.SMEM), vmem, vmem],
        out_specs=[vmem] * mine.shape[0],
        compiler_params=pltpu.CompilerParams(vmem_limit_bytes=8 * 2**20),
        name="merge",
    )(me, mine, got)


def place_kernel(me_ref, *refs):
    out_ref = refs[-1]
    chips = len(refs) - 1
    chip = lax.div(me_ref[0], 2)
    for k, ref in enumerate(refs[:-1]):
        at = pl.multiple_of(lax.rem(chip - k + chips, chips) * BLOCK, BLOCK)
        out_ref[:, pl.ds(at, BLOCK)] = ref[...]


def place_call(me, parts):
    toks = parts[0].shape[0]
    vmem = pl.BlockSpec(memory_space=pltpu.VMEM)
    return pl.pallas_call(
        place_kernel,
        out_shape=jax.ShapeDtypeStruct((toks, len(parts) * BLOCK), parts[0].dtype),
        in_specs=[pl.BlockSpec(memory_space=pltpu.SMEM)] + [vmem] * len(parts),
        out_specs=vmem,
        compiler_params=pltpu.CompilerParams(vmem_limit_bytes=8 * 2**20),
        name="place",
    )(me, *parts)


def return_heads(me, mine, give):
    peers = lax.axis_size("seq")
    chips = peers // 2
    got = lax.ppermute(give, "seq", [(i, i ^ 1) for i in range(peers)])
    parts = merge_call(me, mine, got)
    here = [parts[0]] + [
        lax.ppermute(parts[k], "seq", [(i, (i + 2 * k) % peers) for i in range(peers)])
        for k in range(1, chips)
    ]
    return place_call(me, here)


def local(volume, cotangent, weights, pairs, valid):
    peers = lax.axis_size("seq")
    owners = lax.axis_size("dp")
    vol, cot = volume[0], cotangent[0]
    toks, width = vol.shape
    w_rows = weights.shape[0]
    half = toks // 2

    me = lax.axis_index("seq").reshape(1)
    gathered = lax.all_gather(vol, "seq", axis=0, tiled=True)

    cot = cot.reshape(2, half, peers, HD).transpose(2, 1, 0, 3).reshape(peers, half, 2 * HD)
    cot = lax.all_to_all(cot, "seq", split_axis=0, concat_axis=0, tiled=True)
    weights, cot = lax.optimization_barrier((weights, cot))

    column = lax.axis_index("seq") * HD
    part = lax.dynamic_slice_in_dim(weights, column, HD, axis=2)
    part = jnp.stack([part[:, 1], part[:, 2], part[:, 0]], axis=1).reshape(-1, BLOCK)
    sent = jnp.broadcast_to(part[None], (owners, *part.shape))
    w = lax.all_to_all(sent, "dp", split_axis=0, concat_axis=0, tiled=True)
    w = w.reshape(owners * w_rows, 3 * HD)
    w = jnp.pad(w, ((0, 0), (0, HD)))

    mine, give, wg = head_call(me, pairs[0, 0], valid[0, 0], w, cot, gathered, owners)

    wg = lax.all_to_all(wg, "dp", split_axis=0, concat_axis=0, tiled=True)
    att = return_heads(me, mine, give)[None]
    total = jnp.sum(wg.astype(jnp.float32), axis=0)
    kv = total[:w_rows].reshape(w_rows, 2, HD)
    q = total[w_rows:].reshape(w_rows // 2, 2, HD).transpose(1, 0, 2).reshape(w_rows, 1, HD)
    return att, jnp.concatenate([q, kv], axis=1)


def solution(mesh):
    return jax.shard_map(
        local,
        mesh=mesh,
        in_specs=(
            P("dp", "seq", None),
            P("dp", "seq", None),
            P("dp", None, None),
            P("dp", "seq", None, None),
            P("dp", "seq", None, None),
        ),
        out_specs=(P("dp", "seq", None), P("dp", None, "seq")),
        check_vma=False,
    )
```

```python
import functools

import jax
import jax.numpy as jnp
from jax import lax
from jax.experimental import pallas as pl
from jax.experimental.pallas import tpu as pltpu
from jax.sharding import PartitionSpec as P

HD = 64
BLOCK = 128
LOG2E = 1.4426950408889634
UNROLL = 6
AHEAD = 6
CHUNKS = 8

NN = (((1,), (0,)), ((), ()))
NT = (((1,), (1,)), ((), ()))


def mm(a, b, dims=NN):
    return lax.dot_general(a, b, dims, preferred_element_type=jnp.float32)


def row(b):
    return pl.ds(pl.multiple_of(b * BLOCK, BLOCK), BLOCK)


def softmax(scores, live):
    parts = [scores[j * BLOCK:(j + 1) * BLOCK] * (HD ** -0.5 * LOG2E) for j in range(len(live))]
    tops = [
        jnp.where(ok, jnp.max(part, axis=0, keepdims=True), -jnp.inf)
        for ok, part in zip(live, parts)
    ]
    top = functools.reduce(jnp.maximum, tops)
    exponent = jnp.concatenate(
        [jnp.exp2(part - jnp.where(ok, top, jnp.inf)) for ok, part in zip(live, parts)], axis=0
    )
    return exponent * (1.0 / jnp.sum(exponent, axis=0, keepdims=True))


def forward_kernel(
    pairs_ref, valid_ref, w_ref, vol_hbm, att_ref, kv_ref, kvt_ref, q_ref, vol_ref, o_ref, sems,
):
    rows = vol_ref.shape[0]
    n_blocks, slots = pairs_ref.shape
    peers, half, _ = att_ref.shape
    chunk = rows // CHUNKS
    copies = [
        pltpu.make_async_copy(
            vol_hbm.at[pl.ds(c * chunk, chunk)], vol_ref.at[pl.ds(c * chunk, chunk)], sems.at[c]
        )
        for c in range(CHUNKS)
    ]
    for copy in copies:
        copy.start()
    for c in range(CHUNKS):
        copies[c].wait()
        at = pl.ds(c * chunk, chunk)
        got = mm(vol_ref[at, :], w_ref[...])
        q_ref[at, :] = got[:, BLOCK:].astype(jnp.bfloat16)
        kv = got[:, :BLOCK].astype(jnp.bfloat16)
        kv_ref[at, :] = kv
        for b in range(chunk // BLOCK):
            kvt_ref[c * (chunk // BLOCK) + b] = kv[b * BLOCK:(b + 1) * BLOCK].T

    def body(i, carry):
        blocks = [i * AHEAD + u for u in range(AHEAD)]
        names = [[pairs_ref[b, j] for j in range(slots)] for b in blocks]
        scores = [
            mm(jnp.concatenate([kv_ref[row(n), :] for n in some], axis=0), q_ref[row(b), :], NT)
            for b, some in zip(blocks, names)
        ]
        probs = [
            softmax(s, [valid_ref[b, j] > 0 for j in range(slots)]).astype(jnp.bfloat16)
            for b, s in zip(blocks, scores)
        ]
        for b, some, p in zip(blocks, names, probs):
            values = jnp.concatenate([kvt_ref[n, HD:] for n in some], axis=1)
            o_ref[row(b), :] = mm(values, p).T.astype(jnp.bfloat16)
        return carry

    lax.fori_loop(0, n_blocks // AHEAD, body, 0)

    for s in range(peers):
        att_ref[s] = jnp.concatenate(
            [
                o_ref[pl.ds(2 * half * s, half), :],
                o_ref[pl.ds(2 * half * s + half, half), :],
            ],
            axis=1,
        )


def forward_call(pairs, valid, w, vol, peers):
    rows, width = vol.shape
    n_blocks = rows // BLOCK
    vmem = pl.BlockSpec(memory_space=pltpu.VMEM)
    smem = pl.BlockSpec(memory_space=pltpu.SMEM)
    return pl.pallas_call(
        forward_kernel,
        out_shape=(
            jax.ShapeDtypeStruct((peers, rows // peers // 2, BLOCK), jnp.bfloat16),
            jax.ShapeDtypeStruct((rows, BLOCK), jnp.bfloat16),
            jax.ShapeDtypeStruct((n_blocks, BLOCK, BLOCK), jnp.bfloat16),
            jax.ShapeDtypeStruct((rows, BLOCK), jnp.bfloat16),
        ),
        in_specs=[smem] * 2 + [vmem, pl.BlockSpec(memory_space=pl.ANY)],
        out_specs=(vmem,) * 4,
        scratch_shapes=[
            pltpu.VMEM((rows, width), jnp.bfloat16),
            pltpu.VMEM((rows, HD), jnp.bfloat16),
            pltpu.SemaphoreType.DMA((CHUNKS,)),
        ],
        compiler_params=pltpu.CompilerParams(vmem_limit_bytes=56 * 2**20),
        name="forward",
    )(pairs, valid, w, vol)


def backward_kernel(
    pairs_ref, valid_ref, cot_ref, kv_ref, kvt_ref, q_ref, vol_hbm, wg_ref,
    vol_ref, do_ref, acc_ref, dt_ref, sem,
):
    rows, width = vol_ref.shape
    n_blocks, slots = pairs_ref.shape
    peers, half, _ = cot_ref.shape
    scale = HD ** -0.5
    copy = pltpu.make_async_copy(vol_hbm, vol_ref, sem)
    copy.start()

    acc_ref[...] = jnp.zeros_like(acc_ref)
    blank = jnp.zeros((half, HD), jnp.bfloat16)
    for s in range(peers):
        both = cot_ref[s]
        do_ref[pl.ds(2 * half * s, half), :] = jnp.concatenate([blank, both[:, :HD]], axis=1)
        do_ref[pl.ds(2 * half * s + half, half), :] = jnp.concatenate([blank, both[:, HD:]], axis=1)

    def body(i, carry):
        blocks = [i * UNROLL + u for u in range(UNROLL)]
        names = [[pairs_ref[b, j] for j in range(slots)] for b in blocks]
        rhs = [jnp.concatenate([q_ref[row(b), :], do_ref[row(b), :]], axis=0) for b in blocks]
        both = [
            mm(jnp.concatenate([kv_ref[row(n), :] for n in some], axis=0), r, NT)
            for some, r in zip(names, rhs)
        ]
        sent = []
        for b, pair in zip(blocks, both):
            probs = softmax(pair[:, :BLOCK], [valid_ref[b, j] > 0 for j in range(slots)])
            weighted = probs * pair[:, BLOCK:]
            row_dot = jnp.sum(weighted, axis=0, keepdims=True)
            score_grad = (weighted - probs * row_dot).astype(jnp.bfloat16)
            sent.append((score_grad, probs.astype(jnp.bfloat16)))
        for b, some, pair in zip(blocks, names, sent):
            keys = jnp.concatenate([kvt_ref[n, :HD] for n in some], axis=1)
            dt_ref[BLOCK:, row(b)] = (mm(keys, pair[0]) * scale).astype(jnp.bfloat16)
        for some, pair, r in zip(names, sent, rhs):
            back = mm(jnp.concatenate(pair, axis=1), r)
            for j in range(slots):
                acc_ref[some[j]] += back[j * BLOCK:(j + 1) * BLOCK]
        return carry

    lax.fori_loop(0, n_blocks // UNROLL, body, 0)

    lane = lax.broadcasted_iota(jnp.int32, (BLOCK, BLOCK), 1)
    factor = jnp.where(lane < HD, scale, 1.0)
    for b in range(n_blocks):
        dt_ref[:BLOCK, b * BLOCK:(b + 1) * BLOCK] = (acc_ref[b] * factor).T.astype(jnp.bfloat16)

    copy.wait()
    owners = wg_ref.shape[0]
    mine = width // owners
    part = 256
    for n in range(width // part):
        got = mm(dt_ref[...], vol_ref[:, n * part:(n + 1) * part])
        kv_part = got[:BLOCK].T.astype(jnp.bfloat16)
        q_part = got[BLOCK:].T.astype(jnp.bfloat16)
        for k in range(part // mine):
            owner = n * (part // mine) + k
            wg_ref[owner, :mine] = kv_part[k * mine:(k + 1) * mine]
            q_rows = q_part[k * mine:(k + 1) * mine]
            wg_ref[owner, mine:] = jnp.concatenate([q_rows[:mine // 2], q_rows[mine // 2:]], axis=1)


def backward_call(pairs, valid, cot, kv, kvt, q, vol, owners):
    rows, width = vol.shape
    n_blocks = rows // BLOCK
    mine = width // owners
    vmem = pl.BlockSpec(memory_space=pltpu.VMEM)
    smem = pl.BlockSpec(memory_space=pltpu.SMEM)
    return pl.pallas_call(
        backward_kernel,
        out_shape=jax.ShapeDtypeStruct((owners, mine + mine // 2, BLOCK), jnp.bfloat16),
        in_specs=[smem] * 2 + [vmem] * 4 + [pl.BlockSpec(memory_space=pl.ANY)],
        out_specs=vmem,
        scratch_shapes=[
            pltpu.VMEM((rows, width), jnp.bfloat16),
            pltpu.VMEM((rows, BLOCK), jnp.bfloat16),
            pltpu.VMEM((n_blocks, BLOCK, BLOCK), jnp.float32),
            pltpu.VMEM((BLOCK + HD, rows), jnp.bfloat16),
            pltpu.SemaphoreType.DMA,
        ],
        compiler_params=pltpu.CompilerParams(vmem_limit_bytes=56 * 2**20),
        cost_estimate=pl.CostEstimate(
            flops=12 * 10**9, bytes_accessed=20 * 2**20, transcendentals=n_blocks * 2**16
        ),
        name="backward",
    )(pairs, valid, cot, kv, kvt, q, vol)


def place_kernel(got_ref, out_ref):
    peers, half, _ = got_ref.shape
    for p in range(peers // 2):
        one, two = got_ref[2 * p], got_ref[2 * p + 1]
        at = pl.ds(p * BLOCK, BLOCK)
        out_ref[:half, at] = jnp.concatenate([one[:, :HD], two[:, :HD]], axis=1)
        out_ref[half:, at] = jnp.concatenate([one[:, HD:], two[:, HD:]], axis=1)


def place_call(got):
    peers, half, _ = got.shape
    vmem = pl.BlockSpec(memory_space=pltpu.VMEM)
    return pl.pallas_call(
        place_kernel,
        out_shape=jax.ShapeDtypeStruct((2 * half, peers * HD), got.dtype),
        in_specs=[vmem],
        out_specs=vmem,
        compiler_params=pltpu.CompilerParams(vmem_limit_bytes=8 * 2**20),
        name="place",
    )(got)


def total_kernel(got_ref, out_ref):
    mine = out_ref.shape[1]
    total = got_ref[0].astype(jnp.float32)
    for i in range(1, got_ref.shape[0]):
        total += got_ref[i].astype(jnp.float32)
    out_ref[0, :mine // 2] = total[mine:, :HD]
    out_ref[0, mine // 2:] = total[mine:, HD:]
    out_ref[1] = total[:mine, :HD]
    out_ref[2] = total[:mine, HD:]


def total_call(got, mine):
    vmem = pl.BlockSpec(memory_space=pltpu.VMEM)
    return pl.pallas_call(
        total_kernel,
        out_shape=jax.ShapeDtypeStruct((3, mine, HD), jnp.float32),
        in_specs=[vmem],
        out_specs=vmem,
        compiler_params=pltpu.CompilerParams(vmem_limit_bytes=8 * 2**20),
        name="total",
    )(got)


def local(volume, cotangent, weights, pairs, valid):
    peers = lax.axis_size("seq")
    owners = lax.axis_size("dp")
    vol, cot = volume[0], cotangent[0]
    toks, width = vol.shape
    w_rows = weights.shape[0]
    half = toks // 2

    gathered = lax.all_gather(vol, "seq", axis=0, tiled=True)

    cot = cot.reshape(2, half, peers, HD).transpose(2, 1, 0, 3).reshape(peers, half, 2 * HD)
    cot = lax.all_to_all(cot, "seq", split_axis=0, concat_axis=0, tiled=True)
    weights, cot = lax.optimization_barrier((weights, cot))

    column = lax.axis_index("seq") * HD
    part = lax.dynamic_slice_in_dim(weights, column, HD, axis=2)
    part = jnp.stack([part[:, 1], part[:, 2], part[:, 0]], axis=1).reshape(-1, BLOCK)
    sent = jnp.broadcast_to(part[None], (owners, *part.shape))
    w = lax.all_to_all(sent, "dp", split_axis=0, concat_axis=0, tiled=True)
    w = w.reshape(owners * w_rows, 3 * HD)
    w = jnp.pad(w, ((0, 0), (0, HD)))

    pairs, valid = pairs[0, 0], valid[0, 0]
    att, kv, kvt, q = forward_call(pairs, valid, w, gathered, peers)
    att = lax.all_to_all(att, "seq", split_axis=0, concat_axis=0, tiled=True)
    wg = backward_call(pairs, valid, cot, kv, kvt, q, gathered, owners)
    att = place_call(att)
    wg, att = lax.optimization_barrier((wg, att))
    wg = lax.all_to_all(wg, "dp", split_axis=0, concat_axis=0, tiled=True)
    return att[None], total_call(wg, w_rows).transpose(1, 0, 2)


def solution(mesh):
    return jax.shard_map(
        local,
        mesh=mesh,
        in_specs=(
            P("dp", "seq", None),
            P("dp", "seq", None),
            P("dp", None, None),
            P("dp", "seq", None, None),
            P("dp", "seq", None, None),
        ),
        out_specs=(P("dp", "seq", None), P("dp", None, "seq")),
        check_vma=False,
    )
```

```python
import functools

import jax
import jax.numpy as jnp
from jax import lax
from jax.experimental import pallas as pl
from jax.experimental.pallas import tpu as pltpu
from jax.sharding import PartitionSpec as P

HD = 64
BLOCK = 128
LOG2E = 1.4426950408889634
UNROLL = 6
AHEAD = 6

NN = (((1,), (0,)), ((), ()))
NT = (((1,), (1,)), ((), ()))


def mm(a, b, dims=NN):
    return lax.dot_general(a, b, dims, preferred_element_type=jnp.float32)


def row(b):
    return pl.ds(pl.multiple_of(b * BLOCK, BLOCK), BLOCK)


def softmax(scores, live):
    parts = [scores[j * BLOCK:(j + 1) * BLOCK] * (HD ** -0.5 * LOG2E) for j in range(len(live))]
    tops = [
        jnp.where(ok, jnp.max(part, axis=0, keepdims=True), -jnp.inf)
        for ok, part in zip(live, parts)
    ]
    top = functools.reduce(jnp.maximum, tops)
    exponent = jnp.concatenate(
        [jnp.exp2(part - jnp.where(ok, top, jnp.inf)) for ok, part in zip(live, parts)], axis=0
    )
    return exponent * (1.0 / jnp.sum(exponent, axis=0, keepdims=True))


def block_places(me, peers):
    core = lax.rem(me, 2)
    chip = lax.div(me, 2)
    chips = peers // 2
    ahead = 1 - 2 * core
    places = [me, me + ahead]
    for k in range(1, chips // 2 + 1):
        back = lax.rem(chip - k * ahead + chips, chips)
        forth = lax.rem(chip + k * ahead + chips, chips)
        places += [2 * back + core, 2 * forth + 1 - core]
        if k < chips // 2:
            places += [2 * back + 1 - core, 2 * forth + core]
    return places


def forward_kernel(*refs):
    me_ref, pairs_ref, valid_ref, got_ref = refs[:4]
    att_ref, kv_ref, kvt_ref, q_ref, held_ref, w_ref, o_ref, sems = refs[-8:]
    blocks = refs[4:-8]
    toks = blocks[0].shape[0]
    copies = [
        pltpu.make_async_copy(block_ref, held_ref.at[c], sems.at[c])
        for c, block_ref in enumerate(blocks)
    ]
    for copy in copies:
        copy.start()
    n_blocks, slots = pairs_ref.shape
    peers, half, _ = att_ref.shape
    depth = got_ref.shape[1] // 2
    for s in range(got_ref.shape[0]):
        w_ref[pl.ds(s * depth, depth), :] = jnp.concatenate([got_ref[s, :depth], got_ref[s, depth:]], axis=1)
    for c, place in enumerate(block_places(me_ref[0], peers)):
        at = pl.ds(pl.multiple_of(place * toks, HD), toks)
        copies[c].wait()
        got = mm(held_ref[c], w_ref[...])
        q_ref[at, :] = got[:, BLOCK:].astype(jnp.bfloat16)
        kv_ref[at, :] = got[:, :BLOCK].astype(jnp.bfloat16)
    for b in range(n_blocks):
        kvt_ref[b] = kv_ref[b * BLOCK:(b + 1) * BLOCK, :].T

    def body(i, carry):
        blocks = [i * AHEAD + u for u in range(AHEAD)]
        names = [[pairs_ref[b, j] for j in range(slots)] for b in blocks]
        scores = [
            mm(jnp.concatenate([kv_ref[row(n), :] for n in some], axis=0), q_ref[row(b), :], NT)
            for b, some in zip(blocks, names)
        ]
        probs = [
            softmax(s, [valid_ref[b, j] > 0 for j in range(slots)]).astype(jnp.bfloat16)
            for b, s in zip(blocks, scores)
        ]
        for b, some, p in zip(blocks, names, probs):
            values = jnp.concatenate([kvt_ref[n, HD:] for n in some], axis=1)
            o_ref[row(b), :] = mm(values, p).T.astype(jnp.bfloat16)
        return carry

    lax.fori_loop(0, n_blocks // AHEAD, body, 0)

    for s in range(peers):
        att_ref[s] = jnp.concatenate(
            [
                o_ref[pl.ds(2 * half * s, half), :],
                o_ref[pl.ds(2 * half * s + half, half), :],
            ],
            axis=1,
        )


def forward_call(me, pairs, valid, w, blocks):
    peers = len(blocks)
    toks, width = blocks[0].shape
    rows = toks * peers
    n_blocks = rows // BLOCK
    vmem = pl.BlockSpec(memory_space=pltpu.VMEM)
    smem = pl.BlockSpec(memory_space=pltpu.SMEM)
    return pl.pallas_call(
        forward_kernel,
        out_shape=(
            jax.ShapeDtypeStruct((peers, toks // 2, BLOCK), jnp.bfloat16),
            jax.ShapeDtypeStruct((rows, BLOCK), jnp.bfloat16),
            jax.ShapeDtypeStruct((n_blocks, BLOCK, BLOCK), jnp.bfloat16),
            jax.ShapeDtypeStruct((rows, BLOCK), jnp.bfloat16),
        ),
        in_specs=[smem] * 3 + [vmem] + [pl.BlockSpec(memory_space=pl.ANY)] * peers,
        out_specs=(vmem,) * 4,
        scratch_shapes=[
            pltpu.VMEM((peers, toks, width), jnp.bfloat16),
            pltpu.VMEM((width, 2 * BLOCK), jnp.bfloat16),
            pltpu.VMEM((rows, HD), jnp.bfloat16),
            pltpu.SemaphoreType.DMA((peers,)),
        ],
        compiler_params=pltpu.CompilerParams(vmem_limit_bytes=56 * 2**20),
        name="forward",
    )(me, pairs, valid, w, *blocks)


def backward_kernel(*refs):
    me_ref, pairs_ref, valid_ref, cot_ref, kv_ref, kvt_ref, q_ref = refs[:7]
    wg_ref, vol_ref, do_ref, acc_ref, dt_ref, sems = refs[-6:]
    blocks = refs[7:-6]
    width = vol_ref.shape[1]
    n_blocks, slots = pairs_ref.shape
    peers, half, _ = cot_ref.shape
    scale = HD ** -0.5
    copies = [
        pltpu.make_async_copy(
            block_ref,
            vol_ref.at[pl.ds(pl.multiple_of(place * (2 * half), HD), 2 * half)],
            sems.at[c],
        )
        for c, (place, block_ref) in enumerate(zip(block_places(me_ref[0], peers), blocks))
    ]
    for copy in copies:
        copy.start()

    acc_ref[...] = jnp.zeros_like(acc_ref)
    blank = jnp.zeros((half, HD), jnp.bfloat16)
    for s in range(peers):
        both = cot_ref[s]
        do_ref[pl.ds(2 * half * s, half), :] = jnp.concatenate([blank, both[:, :HD]], axis=1)
        do_ref[pl.ds(2 * half * s + half, half), :] = jnp.concatenate([blank, both[:, HD:]], axis=1)

    def body(i, carry):
        blocks = [i * UNROLL + u for u in range(UNROLL)]
        names = [[pairs_ref[b, j] for j in range(slots)] for b in blocks]
        rhs = [jnp.concatenate([q_ref[row(b), :], do_ref[row(b), :]], axis=0) for b in blocks]
        both = [
            mm(jnp.concatenate([kv_ref[row(n), :] for n in some], axis=0), r, NT)
            for some, r in zip(names, rhs)
        ]
        sent = []
        for b, pair in zip(blocks, both):
            probs = softmax(pair[:, :BLOCK], [valid_ref[b, j] > 0 for j in range(slots)])
            weighted = probs * pair[:, BLOCK:]
            row_dot = jnp.sum(weighted, axis=0, keepdims=True)
            score_grad = (weighted - probs * row_dot).astype(jnp.bfloat16)
            sent.append((score_grad, probs.astype(jnp.bfloat16)))
        for b, some, pair in zip(blocks, names, sent):
            keys = jnp.concatenate([kvt_ref[n, :HD] for n in some], axis=1)
            dt_ref[BLOCK:, row(b)] = (mm(keys, pair[0]) * scale).astype(jnp.bfloat16)
        for some, pair, r in zip(names, sent, rhs):
            back = mm(jnp.concatenate(pair, axis=1), r)
            for j in range(slots):
                acc_ref[some[j]] += back[j * BLOCK:(j + 1) * BLOCK]
        return carry

    lax.fori_loop(0, n_blocks // UNROLL, body, 0)

    lane = lax.broadcasted_iota(jnp.int32, (BLOCK, BLOCK), 1)
    factor = jnp.where(lane < HD, scale, 1.0)
    for b in range(n_blocks):
        dt_ref[:BLOCK, b * BLOCK:(b + 1) * BLOCK] = (acc_ref[b] * factor).T.astype(jnp.bfloat16)

    for copy in copies:
        copy.wait()
    owners = wg_ref.shape[0]
    mine = width // owners
    part = 256
    for n in range(width // part):
        got = mm(dt_ref[...], vol_ref[:, n * part:(n + 1) * part])
        kv_part = got[:BLOCK].T.astype(jnp.bfloat16)
        q_part = got[BLOCK:].T.astype(jnp.bfloat16)
        for k in range(part // mine):
            owner = n * (part // mine) + k
            wg_ref[owner, :mine] = kv_part[k * mine:(k + 1) * mine]
            q_rows = q_part[k * mine:(k + 1) * mine]
            wg_ref[owner, mine:] = jnp.concatenate([q_rows[:mine // 2], q_rows[mine // 2:]], axis=1)


def backward_call(me, pairs, valid, cot, kv, kvt, q, blocks, owners):
    toks, width = blocks[0].shape
    rows = toks * len(blocks)
    n_blocks = rows // BLOCK
    mine = width // owners
    vmem = pl.BlockSpec(memory_space=pltpu.VMEM)
    smem = pl.BlockSpec(memory_space=pltpu.SMEM)
    return pl.pallas_call(
        backward_kernel,
        out_shape=jax.ShapeDtypeStruct((owners, mine + mine // 2, BLOCK), jnp.bfloat16),
        in_specs=[smem] * 3 + [vmem] * 4 + [pl.BlockSpec(memory_space=pl.ANY)] * len(blocks),
        out_specs=vmem,
        scratch_shapes=[
            pltpu.VMEM((rows, width), jnp.bfloat16),
            pltpu.VMEM((rows, BLOCK), jnp.bfloat16),
            pltpu.VMEM((n_blocks, BLOCK, BLOCK), jnp.float32),
            pltpu.VMEM((BLOCK + HD, rows), jnp.bfloat16),
            pltpu.SemaphoreType.DMA((len(blocks),)),
        ],
        compiler_params=pltpu.CompilerParams(vmem_limit_bytes=56 * 2**20),
        cost_estimate=pl.CostEstimate(
            flops=12 * 10**9, bytes_accessed=20 * 2**20, transcendentals=n_blocks * 2**16
        ),
        name="backward",
    )(me, pairs, valid, cot, kv, kvt, q, *blocks)


def place_kernel(got_ref, out_ref):
    peers, half, _ = got_ref.shape
    for p in range(peers // 2):
        one, two = got_ref[2 * p], got_ref[2 * p + 1]
        at = pl.ds(p * BLOCK, BLOCK)
        out_ref[:half, at] = jnp.concatenate([one[:, :HD], two[:, :HD]], axis=1)
        out_ref[half:, at] = jnp.concatenate([one[:, HD:], two[:, HD:]], axis=1)


def place_call(got):
    peers, half, _ = got.shape
    vmem = pl.BlockSpec(memory_space=pltpu.VMEM)
    return pl.pallas_call(
        place_kernel,
        out_shape=jax.ShapeDtypeStruct((2 * half, peers * HD), got.dtype),
        in_specs=[vmem],
        out_specs=vmem,
        compiler_params=pltpu.CompilerParams(vmem_limit_bytes=8 * 2**20),
        name="place",
    )(got)


def total_kernel(got_ref, out_ref):
    mine = out_ref.shape[1]
    total = got_ref[0].astype(jnp.float32)
    for i in range(1, got_ref.shape[0]):
        total += got_ref[i].astype(jnp.float32)
    out_ref[0, :mine // 2] = total[mine:, :HD]
    out_ref[0, mine // 2:] = total[mine:, HD:]
    out_ref[1] = total[:mine, :HD]
    out_ref[2] = total[:mine, HD:]


def total_call(got, mine):
    vmem = pl.BlockSpec(memory_space=pltpu.VMEM)
    return pl.pallas_call(
        total_kernel,
        out_shape=jax.ShapeDtypeStruct((3, mine, HD), jnp.float32),
        in_specs=[vmem],
        out_specs=vmem,
        compiler_params=pltpu.CompilerParams(vmem_limit_bytes=8 * 2**20),
        name="total",
    )(got)


def pack_weights_kernel(me_ref, weights_ref, out_ref):
    core = lax.rem(me_ref[0], 2)
    at = pl.ds(pl.multiple_of(lax.div(me_ref[0], 2) * BLOCK, BLOCK), BLOCK)
    depth = weights_ref.shape[1]
    q, k, v = (weights_ref[t, :, at] for t in range(3))
    blank = jnp.zeros((depth, HD), q.dtype)

    def side(half):
        kv = jnp.concatenate([half(k), half(v)], axis=1)
        return jnp.concatenate([kv, jnp.concatenate([half(q), blank], axis=1)], axis=0)

    one = jnp.where(core == 0, side(lambda x: x[:, :HD]), side(lambda x: x[:, HD:]))
    for i in range(out_ref.shape[0]):
        out_ref[i] = one


def pack_weights(me, weights, owners):
    depth = weights.shape[0]
    vmem = pl.BlockSpec(memory_space=pltpu.VMEM)
    return pl.pallas_call(
        pack_weights_kernel,
        out_shape=jax.ShapeDtypeStruct((owners, 2 * depth, BLOCK), weights.dtype),
        in_specs=[pl.BlockSpec(memory_space=pltpu.SMEM), vmem],
        out_specs=vmem,
        compiler_params=pltpu.CompilerParams(vmem_limit_bytes=8 * 2**20),
        name="pack_weights",
    )(me, weights.transpose(1, 0, 2))


def pack_cotangent_kernel(cot_ref, out_ref):
    peers, half, _ = out_ref.shape
    for p in range(peers // 2):
        at = pl.ds(p * BLOCK, BLOCK)
        first, second = cot_ref[:half, at], cot_ref[half:, at]
        out_ref[2 * p] = jnp.concatenate([first[:, :HD], second[:, :HD]], axis=1)
        out_ref[2 * p + 1] = jnp.concatenate([first[:, HD:], second[:, HD:]], axis=1)


def pack_cotangent(cot, peers):
    toks = cot.shape[0]
    vmem = pl.BlockSpec(memory_space=pltpu.VMEM)
    return pl.pallas_call(
        pack_cotangent_kernel,
        out_shape=jax.ShapeDtypeStruct((peers, toks // 2, BLOCK), cot.dtype),
        in_specs=[vmem],
        out_specs=vmem,
        compiler_params=pltpu.CompilerParams(vmem_limit_bytes=8 * 2**20),
        name="pack_cotangent",
    )(cot)


def gather(vol):
    peers = lax.axis_size("seq")
    chips = peers // 2
    onward = [
        (2 * z + c, 2 * ((z + 1) % chips) if c == 0 else 2 * ((z - 1) % chips) + 1)
        for z in range(chips)
        for c in range(2)
    ]
    twin = [(i, i ^ 1) for i in range(peers)]

    def swap(x):
        return lax.ppermute(x, "seq", twin)

    own, other = vol, swap(vol)
    blocks = [own, other]
    last = chips // 2
    for k in range(1, last + 1):
        if k >= 3:
            n = 4 * (k - 2) + 1
            own, other, blocks[n], blocks[n - 2] = lax.optimization_barrier(
                (own, other, blocks[n], blocks[n - 2])
            )
        own = lax.ppermute(own, "seq", onward)
        if k < last:
            other = lax.ppermute(other, "seq", onward)
        blocks += [own, swap(own)]
        if k < last:
            blocks += [other, swap(other)]
    return blocks


def local(volume, cotangent, weights, pairs, valid):
    peers = lax.axis_size("seq")
    owners = lax.axis_size("dp")
    vol, cot = volume[0], cotangent[0]
    me = lax.axis_index("seq").reshape(1)
    w_rows = weights.shape[0]

    w = lax.all_to_all(pack_weights(me, weights, owners), "dp", split_axis=0, concat_axis=0, tiled=True)
    cot, w = lax.optimization_barrier((cot, w))
    cot = lax.all_to_all(pack_cotangent(cot, peers), "seq", split_axis=0, concat_axis=0, tiled=True)
    blocks = gather(vol)

    pairs, valid = pairs[0, 0], valid[0, 0]
    att, kv, kvt, q = forward_call(me, pairs, valid, w, blocks)
    att = lax.all_to_all(att, "seq", split_axis=0, concat_axis=0, tiled=True)
    wg = backward_call(me, pairs, valid, cot, kv, kvt, q, blocks, owners)
    att = place_call(att)
    wg, att = lax.optimization_barrier((wg, att))
    wg = lax.all_to_all(wg, "dp", split_axis=0, concat_axis=0, tiled=True)
    return att[None], total_call(wg, w_rows).transpose(1, 0, 2)


def solution(mesh):
    return jax.shard_map(
        local,
        mesh=mesh,
        in_specs=(
            P("dp", "seq", None),
            P("dp", "seq", None),
            P("dp", None, None),
            P("dp", "seq", None, None),
            P("dp", "seq", None, None),
        ),
        out_specs=(P("dp", "seq", None), P("dp", None, "seq")),
        check_vma=False,
    )
```

```python
import functools

import jax
import jax.numpy as jnp
from jax import lax
from jax.experimental import pallas as pl
from jax.experimental.pallas import tpu as pltpu
from jax.sharding import PartitionSpec as P

HD = 64
BLOCK = 128
LOG2E = 1.4426950408889634
UNROLL = 12
AHEAD = 12
CHUNKS = 6
FLIGHT = 6

NN = (((1,), (0,)), ((), ()))
NT = (((1,), (1,)), ((), ()))


def mm(a, b, dims=NN):
    return lax.dot_general(a, b, dims, preferred_element_type=jnp.float32)


def row(b):
    return pl.ds(pl.multiple_of(b * BLOCK, BLOCK), BLOCK)


def softmax(scores, live):
    parts = [scores[j * BLOCK:(j + 1) * BLOCK] * (HD ** -0.5 * LOG2E) for j in range(len(live))]
    tops = [
        jnp.where(ok, jnp.max(part, axis=0, keepdims=True), -jnp.inf)
        for ok, part in zip(live, parts)
    ]
    top = functools.reduce(jnp.maximum, tops)
    exponent = jnp.concatenate(
        [jnp.exp2(part - jnp.where(ok, top, jnp.inf)) for ok, part in zip(live, parts)], axis=0
    )
    return exponent * (1.0 / jnp.sum(exponent, axis=0, keepdims=True))


def forward_kernel(
    pairs_ref, valid_ref, w_ref, vol_hbm, att_ref, kv_hbm, kvt_hbm, q_hbm,
    vol_ref, kv_ref, kvt_ref, q_ref, in_sems, out_sems,
):
    rows = vol_ref.shape[0]
    n_blocks, slots = pairs_ref.shape
    half = att_ref.shape[1]
    chunk = rows // CHUNKS
    copies = [
        pltpu.make_async_copy(
            vol_hbm.at[pl.ds(c * chunk, chunk)], vol_ref.at[pl.ds(c * chunk, chunk)], in_sems.at[c]
        )
        for c in range(CHUNKS)
    ]
    for copy in copies[:FLIGHT]:
        copy.start()
    for c in range(CHUNKS):
        copies[c].wait()
        if c + FLIGHT < CHUNKS:
            copies[c + FLIGHT].start()
        at = pl.ds(c * chunk, chunk)
        got = mm(vol_ref[at, :], w_ref[...])
        q_ref[at, :] = got[:, BLOCK:].astype(jnp.bfloat16)
        kv = got[:, :BLOCK].astype(jnp.bfloat16)
        kv_ref[at, :] = kv
        for b in range(chunk // BLOCK):
            kvt_ref[c * (chunk // BLOCK) + b] = kv[b * BLOCK:(b + 1) * BLOCK].T
    kept = [
        pltpu.make_async_copy(ref, hbm, out_sems.at[i])
        for i, (ref, hbm) in enumerate(((kv_ref, kv_hbm), (kvt_ref, kvt_hbm), (q_ref, q_hbm)))
    ]
    for copy in kept:
        copy.start()

    def body(i, carry):
        blocks = [i * AHEAD + u for u in range(AHEAD)]
        names = [[pairs_ref[b, j] for j in range(slots)] for b in blocks]
        scores = [
            mm(jnp.concatenate([kv_ref[row(n), :] for n in some], axis=0), q_ref[row(b), :], NT)
            for b, some in zip(blocks, names)
        ]
        probs = [
            softmax(s, [valid_ref[b, j] > 0 for j in range(slots)]).astype(jnp.bfloat16)
            for b, s in zip(blocks, scores)
        ]
        outs = []
        for b, some, p in zip(blocks, names, probs):
            values = jnp.concatenate([kvt_ref[n, HD:] for n in some], axis=1)
            out_t = mm(values, p)
            both = jnp.concatenate([out_t, out_t], axis=0).T.astype(jnp.bfloat16)
            outs.append(both)
        for g in range(AHEAD // 3):
            tokens = jnp.concatenate(outs[3 * g:3 * g + 3], axis=0)
            for h in range(4):
                span = tokens[h * half:(h + 1) * half]
                side = slice(HD * (h % 2), HD * (h % 2) + HD)
                att_ref[(i * (AHEAD // 3) + g) * 2 + h // 2, :, side] = span[:, side]
        return carry

    lax.fori_loop(0, n_blocks // AHEAD, body, 0)
    for copy in kept:
        copy.wait()


def forward_call(pairs, valid, w, vol, peers):
    rows, width = vol.shape
    n_blocks = rows // BLOCK
    vmem = pl.BlockSpec(memory_space=pltpu.VMEM)
    smem = pl.BlockSpec(memory_space=pltpu.SMEM)
    hbm = pl.BlockSpec(memory_space=pl.ANY)
    flat = jax.ShapeDtypeStruct((rows, BLOCK), jnp.bfloat16)
    square = jax.ShapeDtypeStruct((n_blocks, BLOCK, BLOCK), jnp.bfloat16)
    return pl.pallas_call(
        forward_kernel,
        out_shape=(
            jax.ShapeDtypeStruct((peers, rows // peers // 2, BLOCK), jnp.bfloat16),
            flat,
            square,
            flat,
        ),
        in_specs=[smem] * 2 + [vmem, hbm],
        out_specs=(vmem, hbm, hbm, hbm),
        scratch_shapes=[
            pltpu.VMEM((rows, width), jnp.bfloat16),
            pltpu.VMEM(flat.shape, flat.dtype),
            pltpu.VMEM(square.shape, square.dtype),
            pltpu.VMEM(flat.shape, flat.dtype),
            pltpu.SemaphoreType.DMA((CHUNKS,)),
            pltpu.SemaphoreType.DMA((3,)),
        ],
        compiler_params=pltpu.CompilerParams(vmem_limit_bytes=56 * 2**20),
        name="forward",
    )(pairs, valid, w, vol)


def spread_kernel(cot_ref, out_ref):
    peers, half, _ = cot_ref.shape
    blank = jnp.zeros((half, HD), cot_ref.dtype)
    for s in range(peers):
        both = cot_ref[s]
        out_ref[pl.ds(2 * half * s, half), :] = jnp.concatenate([blank, both[:, :HD]], axis=1)
        out_ref[pl.ds(2 * half * s + half, half), :] = jnp.concatenate([blank, both[:, HD:]], axis=1)


def spread_call(cot):
    peers, half, lanes = cot.shape
    vmem = pl.BlockSpec(memory_space=pltpu.VMEM)
    return pl.pallas_call(
        spread_kernel,
        out_shape=jax.ShapeDtypeStruct((2 * half * peers, lanes), cot.dtype),
        in_specs=[vmem],
        out_specs=vmem,
        compiler_params=pltpu.CompilerParams(vmem_limit_bytes=8 * 2**20),
        name="spread",
    )(cot)


def backward_kernel(
    pairs_ref, valid_ref, do_hbm, kv_hbm, kvt_hbm, q_hbm, vol_hbm, wg_ref,
    do_ref, kv_ref, kvt_ref, q_ref, vol_ref, acc_ref, dt_ref, sems,
):
    width = vol_ref.shape[1]
    n_blocks, slots = pairs_ref.shape
    scale = HD ** -0.5
    copies = [
        pltpu.make_async_copy(hbm, ref, sems.at[i])
        for i, (hbm, ref) in enumerate(
            ((kv_hbm, kv_ref), (q_hbm, q_ref), (do_hbm, do_ref), (kvt_hbm, kvt_ref), (vol_hbm, vol_ref))
        )
    ]
    for copy in copies[:-1]:
        copy.start()
    acc_ref[...] = jnp.zeros_like(acc_ref)
    for copy in copies[:-1]:
        copy.wait()
    copies[-1].start()

    def body(i, carry):
        blocks = [i * UNROLL + u for u in range(UNROLL)]
        names = [[pairs_ref[b, j] for j in range(slots)] for b in blocks]
        rhs = [jnp.concatenate([q_ref[row(b), :], do_ref[row(b), :]], axis=0) for b in blocks]
        both = [
            mm(jnp.concatenate([kv_ref[row(n), :] for n in some], axis=0), r, NT)
            for some, r in zip(names, rhs)
        ]
        sent = []
        for b, pair in zip(blocks, both):
            probs = softmax(pair[:, :BLOCK], [valid_ref[b, j] > 0 for j in range(slots)])
            weighted = probs * pair[:, BLOCK:]
            row_dot = jnp.sum(weighted, axis=0, keepdims=True)
            score_grad = (weighted - probs * row_dot).astype(jnp.bfloat16)
            sent.append((score_grad, probs.astype(jnp.bfloat16)))
        for b, some, pair in zip(blocks, names, sent):
            keys = jnp.concatenate([kvt_ref[n, :HD] for n in some], axis=1)
            dt_ref[BLOCK:, row(b)] = (mm(keys, pair[0]) * scale).astype(jnp.bfloat16)
        for some, pair, r in zip(names, sent, rhs):
            back = mm(jnp.concatenate(pair, axis=1), r)
            for j in range(slots):
                acc_ref[some[j]] += back[j * BLOCK:(j + 1) * BLOCK]
        return carry

    lax.fori_loop(0, n_blocks // UNROLL, body, 0)

    lane = lax.broadcasted_iota(jnp.int32, (BLOCK, BLOCK), 1)
    factor = jnp.where(lane < HD, scale, 1.0)
    for b in range(n_blocks):
        dt_ref[:BLOCK, b * BLOCK:(b + 1) * BLOCK] = (acc_ref[b] * factor).astype(jnp.bfloat16).T

    copies[-1].wait()
    owners = wg_ref.shape[0]
    mine = width // owners
    part = 256
    for n in range(width // part):
        got = mm(dt_ref[...], vol_ref[:, n * part:(n + 1) * part]).astype(jnp.bfloat16)
        kv_part = got[:BLOCK].T
        q_part = got[BLOCK:].T
        for k in range(part // mine):
            owner = n * (part // mine) + k
            wg_ref[owner, :mine] = kv_part[k * mine:(k + 1) * mine]
            q_rows = q_part[k * mine:(k + 1) * mine]
            wg_ref[owner, mine:] = jnp.concatenate([q_rows[:mine // 2], q_rows[mine // 2:]], axis=1)


def backward_call(pairs, valid, d_out, kv, kvt, q, vol, owners):
    rows, width = vol.shape
    n_blocks = rows // BLOCK
    mine = width // owners
    vmem = pl.BlockSpec(memory_space=pltpu.VMEM)
    smem = pl.BlockSpec(memory_space=pltpu.SMEM)
    return pl.pallas_call(
        backward_kernel,
        out_shape=jax.ShapeDtypeStruct((owners, mine + mine // 2, BLOCK), jnp.bfloat16),
        in_specs=[smem] * 2 + [pl.BlockSpec(memory_space=pl.ANY)] * 5,
        out_specs=vmem,
        scratch_shapes=[
            pltpu.VMEM((rows, BLOCK), jnp.bfloat16),
            pltpu.VMEM((rows, BLOCK), jnp.bfloat16),
            pltpu.VMEM((n_blocks, BLOCK, BLOCK), jnp.bfloat16),
            pltpu.VMEM((rows, BLOCK), jnp.bfloat16),
            pltpu.VMEM((rows, width), jnp.bfloat16),
            pltpu.VMEM((n_blocks, BLOCK, BLOCK), jnp.float32),
            pltpu.VMEM((BLOCK + HD, rows), jnp.bfloat16),
            pltpu.SemaphoreType.DMA((5,)),
        ],
        compiler_params=pltpu.CompilerParams(vmem_limit_bytes=56 * 2**20),
        cost_estimate=pl.CostEstimate(
            flops=12 * 10**9, bytes_accessed=20 * 2**20, transcendentals=n_blocks * 2**16
        ),
        name="backward",
    )(pairs, valid, d_out, kv, kvt, q, vol)


def finish_kernel(att_ref, wg_ref, out_ref, total_ref):
    mine = total_ref.shape[1]
    total = wg_ref[0].astype(jnp.float32)
    for i in range(1, wg_ref.shape[0]):
        total += wg_ref[i].astype(jnp.float32)
    total_ref[0, :mine // 2] = total[mine:, :HD]
    total_ref[0, mine // 2:] = total[mine:, HD:]
    total_ref[1] = total[:mine, :HD]
    total_ref[2] = total[:mine, HD:]
    peers, half, _ = att_ref.shape
    for p in range(peers // 2):
        one, two = att_ref[2 * p], att_ref[2 * p + 1]
        at = pl.ds(p * BLOCK, BLOCK)
        out_ref[:half, at] = jnp.concatenate([one[:, :HD], two[:, :HD]], axis=1)
        out_ref[half:, at] = jnp.concatenate([one[:, HD:], two[:, HD:]], axis=1)


def finish_call(att, wg, mine):
    peers, half, _ = att.shape
    vmem = pl.BlockSpec(memory_space=pltpu.VMEM)
    return pl.pallas_call(
        finish_kernel,
        out_shape=(
            jax.ShapeDtypeStruct((2 * half, peers * HD), att.dtype),
            jax.ShapeDtypeStruct((3, mine, HD), jnp.float32),
        ),
        in_specs=[vmem] * 2,
        out_specs=(vmem,) * 2,
        compiler_params=pltpu.CompilerParams(vmem_limit_bytes=8 * 2**20),
        name="finish",
    )(att, wg)


def local(volume, cotangent, weights, pairs, valid):
    peers = lax.axis_size("seq")
    owners = lax.axis_size("dp")
    vol, cot = volume[0], cotangent[0]
    toks, width = vol.shape
    w_rows = weights.shape[0]
    half = toks // 2

    gathered = lax.all_gather(vol, "seq", axis=0, tiled=True)

    cot = cot.reshape(2, half, peers, HD).transpose(2, 1, 0, 3).reshape(peers, half, 2 * HD)
    cot = lax.all_to_all(cot, "seq", split_axis=0, concat_axis=0, tiled=True)
    weights, cot = lax.optimization_barrier((weights, cot))
    d_out = spread_call(cot)

    column = lax.axis_index("seq") * HD
    part = lax.dynamic_slice_in_dim(weights, column, HD, axis=2)
    part = jnp.stack([part[:, 1], part[:, 2], part[:, 0]], axis=1).reshape(-1, BLOCK)
    sent = jnp.broadcast_to(part[None], (owners, *part.shape))
    w = lax.all_to_all(sent, "dp", split_axis=0, concat_axis=0, tiled=True)
    w = w.reshape(owners * w_rows, 3 * HD)
    w = jnp.pad(w, ((0, 0), (0, HD)))

    pairs, valid = pairs[0, 0], valid[0, 0]
    att, kv, kvt, q = forward_call(pairs, valid, w, gathered, peers)
    att = lax.all_to_all(att, "seq", split_axis=0, concat_axis=0, tiled=True)
    wg = backward_call(pairs, valid, d_out, kv, kvt, q, gathered, owners)
    wg, att = lax.optimization_barrier((wg, att))
    wg = lax.all_to_all(wg, "dp", split_axis=0, concat_axis=0, tiled=True)
    att, total = finish_call(att, wg, w_rows)
    return att[None], total.transpose(1, 0, 2)


def solution(mesh):
    return jax.shard_map(
        local,
        mesh=mesh,
        in_specs=(
            P("dp", "seq", None),
            P("dp", "seq", None),
            P("dp", None, None),
            P("dp", "seq", None, None),
            P("dp", "seq", None, None),
        ),
        out_specs=(P("dp", "seq", None), P("dp", None, "seq")),
        check_vma=False,
    )
```

```python
import functools

import jax
import jax.numpy as jnp
from jax import lax
from jax.experimental import pallas as pl
from jax.experimental.pallas import tpu as pltpu
from jax.sharding import PartitionSpec as P

HD = 64
BLOCK = 128
LOG2E = 1.4426950408889634
UNROLL = 12
AHEAD = 12
CHUNKS = 1
FLIGHT = 1
PART = 512

NN = (((1,), (0,)), ((), ()))
NT = (((1,), (1,)), ((), ()))


def mm(a, b, dims=NN):
    return lax.dot_general(a, b, dims, preferred_element_type=jnp.float32)


def row(b):
    return pl.ds(pl.multiple_of(b * BLOCK, BLOCK), BLOCK)


def softmax(scores, live):
    parts = [scores[j * BLOCK:(j + 1) * BLOCK] * (HD ** -0.5 * LOG2E) for j in range(len(live))]
    tops = [
        jnp.where(ok, jnp.max(part, axis=0, keepdims=True), -jnp.inf)
        for ok, part in zip(live, parts)
    ]
    top = functools.reduce(jnp.maximum, tops)
    exponent = jnp.concatenate(
        [jnp.exp2(part - jnp.where(ok, top, jnp.inf)) for ok, part in zip(live, parts)], axis=0
    )
    return exponent * (1.0 / jnp.sum(exponent, axis=0, keepdims=True))


def forward_kernel(
    pairs_ref, valid_ref, w_ref, vol_hbm, att_ref, kv_hbm, kt_hbm, q_hbm,
    vol_ref, kv_ref, kt_ref, vt_ref, q_ref, in_sems, out_sems,
):
    rows = vol_ref.shape[0]
    n_blocks, slots = pairs_ref.shape
    half = att_ref.shape[1]
    chunk = rows // CHUNKS
    copies = [
        pltpu.make_async_copy(
            vol_hbm.at[pl.ds(c * chunk, chunk)], vol_ref.at[pl.ds(c * chunk, chunk)], in_sems.at[c]
        )
        for c in range(CHUNKS)
    ]
    for copy in copies[:FLIGHT]:
        copy.start()
    for c in range(CHUNKS):
        copies[c].wait()
        if c + FLIGHT < CHUNKS:
            copies[c + FLIGHT].start()
        at = pl.ds(c * chunk, chunk)
        got = mm(vol_ref[at, :], w_ref[...])
        q_ref[at, :] = got[:, BLOCK:].astype(jnp.bfloat16)
        kv = got[:, :BLOCK].astype(jnp.bfloat16)
        kv_ref[at, :] = kv
        for b in range(chunk // BLOCK):
            turned = kv[b * BLOCK:(b + 1) * BLOCK].T
            kt_ref[c * (chunk // BLOCK) + b] = turned[:HD]
            vt_ref[c * (chunk // BLOCK) + b] = turned[HD:]
    kept = [
        pltpu.make_async_copy(ref, hbm, out_sems.at[i])
        for i, (ref, hbm) in enumerate(((kv_ref, kv_hbm), (kt_ref, kt_hbm), (q_ref, q_hbm)))
    ]
    for copy in kept:
        copy.start()

    def body(i, carry):
        blocks = [i * AHEAD + u for u in range(AHEAD)]
        names = [[pairs_ref[b, j] for j in range(slots)] for b in blocks]
        scores = [
            mm(jnp.concatenate([kv_ref[row(n), :] for n in some], axis=0), q_ref[row(b), :], NT)
            for b, some in zip(blocks, names)
        ]
        probs = [
            softmax(s, [valid_ref[b, j] > 0 for j in range(slots)]).astype(jnp.bfloat16)
            for b, s in zip(blocks, scores)
        ]
        outs = []
        for b, some, p in zip(blocks, names, probs):
            values = jnp.concatenate([vt_ref[n] for n in some], axis=1)
            out_t = mm(values, p)
            both = jnp.concatenate([out_t, out_t], axis=0).T.astype(jnp.bfloat16)
            outs.append(both)
        for g in range(AHEAD // 3):
            tokens = jnp.concatenate(outs[3 * g:3 * g + 3], axis=0)
            for h in range(4):
                span = tokens[h * half:(h + 1) * half]
                side = slice(HD * (h % 2), HD * (h % 2) + HD)
                att_ref[(i * (AHEAD // 3) + g) * 2 + h // 2, :, side] = span[:, side]
        return carry

    lax.fori_loop(0, n_blocks // AHEAD, body, 0)
    for copy in kept:
        copy.wait()


def forward_call(pairs, valid, w, vol, peers):
    rows, width = vol.shape
    n_blocks = rows // BLOCK
    vmem = pl.BlockSpec(memory_space=pltpu.VMEM)
    smem = pl.BlockSpec(memory_space=pltpu.SMEM)
    hbm = pl.BlockSpec(memory_space=pl.ANY)
    flat = jax.ShapeDtypeStruct((rows, BLOCK), jnp.bfloat16)
    turned = jax.ShapeDtypeStruct((n_blocks, HD, BLOCK), jnp.bfloat16)
    return pl.pallas_call(
        forward_kernel,
        out_shape=(
            jax.ShapeDtypeStruct((peers, rows // peers // 2, BLOCK), jnp.bfloat16),
            flat,
            turned,
            flat,
        ),
        in_specs=[smem] * 2 + [vmem, hbm],
        out_specs=(vmem, hbm, hbm, hbm),
        scratch_shapes=[
            pltpu.VMEM((rows, width), jnp.bfloat16),
            pltpu.VMEM(flat.shape, flat.dtype),
            pltpu.VMEM(turned.shape, turned.dtype),
            pltpu.VMEM(turned.shape, turned.dtype),
            pltpu.VMEM(flat.shape, flat.dtype),
            pltpu.SemaphoreType.DMA((CHUNKS,)),
            pltpu.SemaphoreType.DMA((3,)),
        ],
        compiler_params=pltpu.CompilerParams(vmem_limit_bytes=56 * 2**20),
        name="forward",
    )(pairs, valid, w, vol)


def spread_kernel(cot_ref, out_ref):
    peers, half, _ = cot_ref.shape
    blank = jnp.zeros((half, HD), cot_ref.dtype)
    for s in range(peers):
        both = cot_ref[s]
        out_ref[pl.ds(2 * half * s, half), :] = jnp.concatenate([blank, both[:, :HD]], axis=1)
        out_ref[pl.ds(2 * half * s + half, half), :] = jnp.concatenate([blank, both[:, HD:]], axis=1)


def spread_call(cot):
    peers, half, lanes = cot.shape
    vmem = pl.BlockSpec(memory_space=pltpu.VMEM)
    return pl.pallas_call(
        spread_kernel,
        out_shape=jax.ShapeDtypeStruct((2 * half * peers, lanes), cot.dtype),
        in_specs=[vmem],
        out_specs=vmem,
        compiler_params=pltpu.CompilerParams(vmem_limit_bytes=8 * 2**20),
        name="spread",
    )(cot)


def backward_kernel(
    pairs_ref, valid_ref, do_hbm, kv_hbm, kt_hbm, q_hbm, vol_hbm, wg_ref,
    do_ref, kv_ref, kt_ref, q_ref, vol_ref, acc_ref, dt_ref, sems,
):
    width = vol_ref.shape[1]
    n_blocks, slots = pairs_ref.shape
    scale = HD ** -0.5
    copies = [
        pltpu.make_async_copy(hbm, ref, sems.at[i])
        for i, (hbm, ref) in enumerate(
            ((kv_hbm, kv_ref), (q_hbm, q_ref), (do_hbm, do_ref), (kt_hbm, kt_ref), (vol_hbm, vol_ref))
        )
    ]
    for copy in copies[:-1]:
        copy.start()
    acc_ref[...] = jnp.zeros_like(acc_ref)
    for copy in copies[:-1]:
        copy.wait()
    copies[-1].start()

    def body(i, carry):
        blocks = [i * UNROLL + u for u in range(UNROLL)]
        names = [[pairs_ref[b, j] for j in range(slots)] for b in blocks]
        rhs = [jnp.concatenate([q_ref[row(b), :], do_ref[row(b), :]], axis=0) for b in blocks]
        both = [
            mm(jnp.concatenate([kv_ref[row(n), :] for n in some], axis=0), r, NT)
            for some, r in zip(names, rhs)
        ]
        sent = []
        for b, pair in zip(blocks, both):
            probs = softmax(pair[:, :BLOCK], [valid_ref[b, j] > 0 for j in range(slots)])
            weighted = probs * pair[:, BLOCK:]
            row_dot = jnp.sum(weighted, axis=0, keepdims=True)
            score_grad = (weighted - probs * row_dot).astype(jnp.bfloat16)
            sent.append((score_grad, probs.astype(jnp.bfloat16)))
        for b, some, pair in zip(blocks, names, sent):
            keys = jnp.concatenate([kt_ref[n] for n in some], axis=1)
            dt_ref[BLOCK:, row(b)] = (mm(keys, pair[0]) * scale).astype(jnp.bfloat16)
        for some, pair, r in zip(names, sent, rhs):
            back = mm(jnp.concatenate(pair, axis=1), r)
            for j in range(slots):
                acc_ref[some[j]] += back[j * BLOCK:(j + 1) * BLOCK]
        return carry

    lax.fori_loop(0, n_blocks // UNROLL, body, 0)

    lane = lax.broadcasted_iota(jnp.int32, (BLOCK, BLOCK), 1)
    factor = jnp.where(lane < HD, scale, 1.0)
    for b in range(n_blocks):
        dt_ref[:BLOCK, b * BLOCK:(b + 1) * BLOCK] = (acc_ref[b] * factor).astype(jnp.bfloat16).T

    copies[-1].wait()
    owners = wg_ref.shape[0]
    mine = width // owners
    part = PART
    for n in range(width // part):
        got = mm(dt_ref[...], vol_ref[:, n * part:(n + 1) * part]).astype(jnp.bfloat16)
        kv_part = got[:BLOCK].T
        q_part = got[BLOCK:].T
        for k in range(part // mine):
            owner = n * (part // mine) + k
            wg_ref[owner, :mine] = kv_part[k * mine:(k + 1) * mine]
            q_rows = q_part[k * mine:(k + 1) * mine]
            wg_ref[owner, mine:] = jnp.concatenate([q_rows[:mine // 2], q_rows[mine // 2:]], axis=1)


def backward_call(pairs, valid, d_out, kv, kt, q, vol, owners):
    rows, width = vol.shape
    n_blocks = rows // BLOCK
    mine = width // owners
    vmem = pl.BlockSpec(memory_space=pltpu.VMEM)
    smem = pl.BlockSpec(memory_space=pltpu.SMEM)
    return pl.pallas_call(
        backward_kernel,
        out_shape=jax.ShapeDtypeStruct((owners, mine + mine // 2, BLOCK), jnp.bfloat16),
        in_specs=[smem] * 2 + [pl.BlockSpec(memory_space=pl.ANY)] * 5,
        out_specs=vmem,
        scratch_shapes=[
            pltpu.VMEM((rows, BLOCK), jnp.bfloat16),
            pltpu.VMEM((rows, BLOCK), jnp.bfloat16),
            pltpu.VMEM((n_blocks, HD, BLOCK), jnp.bfloat16),
            pltpu.VMEM((rows, BLOCK), jnp.bfloat16),
            pltpu.VMEM((rows, width), jnp.bfloat16),
            pltpu.VMEM((n_blocks, BLOCK, BLOCK), jnp.float32),
            pltpu.VMEM((BLOCK + HD, rows), jnp.bfloat16),
            pltpu.SemaphoreType.DMA((5,)),
        ],
        compiler_params=pltpu.CompilerParams(vmem_limit_bytes=56 * 2**20),
        cost_estimate=pl.CostEstimate(
            flops=12 * 10**9, bytes_accessed=20 * 2**20, transcendentals=n_blocks * 2**16
        ),
        name="backward",
    )(pairs, valid, d_out, kv, kt, q, vol)


def finish_kernel(att_ref, wg_ref, out_ref, total_ref):
    mine = total_ref.shape[1]
    total = wg_ref[0].astype(jnp.float32)
    for i in range(1, wg_ref.shape[0]):
        total += wg_ref[i].astype(jnp.float32)
    total_ref[0, :mine // 2] = total[mine:, :HD]
    total_ref[0, mine // 2:] = total[mine:, HD:]
    total_ref[1] = total[:mine, :HD]
    total_ref[2] = total[:mine, HD:]
    peers, half, _ = att_ref.shape
    for p in range(peers // 2):
        one, two = att_ref[2 * p], att_ref[2 * p + 1]
        at = pl.ds(p * BLOCK, BLOCK)
        out_ref[:half, at] = jnp.concatenate([one[:, :HD], two[:, :HD]], axis=1)
        out_ref[half:, at] = jnp.concatenate([one[:, HD:], two[:, HD:]], axis=1)


def finish_call(att, wg, mine):
    peers, half, _ = att.shape
    vmem = pl.BlockSpec(memory_space=pltpu.VMEM)
    return pl.pallas_call(
        finish_kernel,
        out_shape=(
            jax.ShapeDtypeStruct((2 * half, peers * HD), att.dtype),
            jax.ShapeDtypeStruct((3, mine, HD), jnp.float32),
        ),
        in_specs=[vmem] * 2,
        out_specs=(vmem,) * 2,
        compiler_params=pltpu.CompilerParams(vmem_limit_bytes=8 * 2**20),
        name="finish",
    )(att, wg)


def local(volume, cotangent, weights, pairs, valid):
    peers = lax.axis_size("seq")
    owners = lax.axis_size("dp")
    vol, cot = volume[0], cotangent[0]
    toks, width = vol.shape
    w_rows = weights.shape[0]
    half = toks // 2

    gathered = lax.all_gather(vol, "seq", axis=0, tiled=True)

    cot = cot.reshape(2, half, peers, HD).transpose(2, 1, 0, 3).reshape(peers, half, 2 * HD)
    cot = lax.all_to_all(cot, "seq", split_axis=0, concat_axis=0, tiled=True)
    weights, cot = lax.optimization_barrier((weights, cot))
    d_out = spread_call(cot)

    column = lax.axis_index("seq") * HD
    part = lax.dynamic_slice_in_dim(weights, column, HD, axis=2)
    part = jnp.stack([part[:, 1], part[:, 2], part[:, 0]], axis=1).reshape(-1, BLOCK)
    sent = jnp.broadcast_to(part[None], (owners, *part.shape))
    w = lax.all_to_all(sent, "dp", split_axis=0, concat_axis=0, tiled=True)
    w = w.reshape(owners * w_rows, 3 * HD)
    w = jnp.pad(w, ((0, 0), (0, HD)))

    pairs, valid = pairs[0, 0], valid[0, 0]
    att, kv, kt, q = forward_call(pairs, valid, w, gathered, peers)
    att = lax.all_to_all(att, "seq", split_axis=0, concat_axis=0, tiled=True)
    wg = backward_call(pairs, valid, d_out, kv, kt, q, gathered, owners)
    wg, att = lax.optimization_barrier((wg, att))
    wg = lax.all_to_all(wg, "dp", split_axis=0, concat_axis=0, tiled=True)
    att, total = finish_call(att, wg, w_rows)
    return att[None], total.transpose(1, 0, 2)


def solution(mesh):
    return jax.shard_map(
        local,
        mesh=mesh,
        in_specs=(
            P("dp", "seq", None),
            P("dp", "seq", None),
            P("dp", None, None),
            P("dp", "seq", None, None),
            P("dp", "seq", None, None),
        ),
        out_specs=(P("dp", "seq", None), P("dp", None, "seq")),
        check_vma=False,
    )
```
